32 devices in a mesh: req: 8 (over z, x), tp: 4 (over y, core).
Axes of the slice: x: 2, y: 2, z: 4, core: 2. Of those that a mesh axis runs over, the one named last changes fastest.
Arguments:
- hidden_states: bfloat16 [2048, 2048], P('req'), may hold values from -30 to 30
- norm_gain: float32 [2048], replicated, may hold values from 0.5 to 1.5
- head: bfloat16 [2048, 24576], P(None, ('req', 'tp')), may hold values from -1 to 1
- target_ids: int32 [2048], P('req'), may hold values from 0 to 24575
- lengths: int32 [8], P('req'), may hold values from 32 to 256, as said below
Outputs:
- token_logprob: float32 [2048], P('req')
- token_entropy: float32 [2048], P('req')
- seq_mean_logprob: float32 [8], P('req')
- seq_top_logit: float32 [8], P('req')
The draws below stay inside these ranges and needn't reach their ends.
Inputs may be any that keep to these rules, and one draw needn't show every extreme that they name: `lengths`: each completion has at least 32 and at most 256 live slots; some completion has exactly 256.
All inputs are finite; a program needn't handle non-finite values.
Results may differ from the reference program's by a relative error of at most 0.0018.
Values may be sent and summed in bfloat16 or wider, within the bound.
No kernel may reach another device: no remote copies, remote signals or barrier semaphores. Data moves between devices by JAX's collectives and lax.ppermute only.
A program may use at most 128 MiB of HBM per device.

```python
import math
import jax
import jax.numpy as jnp
import numpy as np
from jax import lax

D = 2048
LMAX = 256
LMIN = 32
NSEQ = 8
TOKENS = 2048
VOCAB = 24576


def draw_hidden_states(key, part):
    base = jax.random.normal(jax.random.fold_in(key, 1), (TOKENS, D), jnp.float32)
    return jnp.clip(base, -30.0, 30.0).astype(jnp.bfloat16)


def draw_head(key, part):
    root = jnp.sqrt(jnp.float32(D))
    noise = jax.random.normal(jax.random.fold_in(key, 3), (D, VOCAB), jnp.float32) * (1.6 / root)
    centers = jax.random.normal(jax.random.fold_in(key, 9), (D, 16), jnp.float32) * (1.2 / root)
    member = jax.random.randint(jax.random.fold_in(key, 10), (VOCAB,), 0, 16, dtype=jnp.int32)
    weights = noise + centers[:, member]
    return jnp.clip(weights, -1.0, 1.0).astype(jnp.bfloat16)


def draw_lengths(key, part):
    lens = jax.random.randint(jax.random.fold_in(key, 5), (NSEQ,), LMIN, LMAX + 1, dtype=jnp.int32)
    where_max = jax.random.randint(jax.random.fold_in(key, 6), (), 0, NSEQ, dtype=jnp.int32)
    return jnp.where(jnp.arange(NSEQ, dtype=jnp.int32) == where_max, jnp.int32(LMAX), lens)


def touch_ends(values, stream_key, smallest, largest):
    longest = values.shape.index(max(values.shape))
    spots = []
    for shift in (0, 1):
        where = [jax.random.randint(jax.random.fold_in(stream_key, axis), (), 0, length) for axis, length in enumerate(values.shape)]
        where[longest] = (where[longest] + shift) % values.shape[longest]
        spots.append(tuple(where))
    return values.at[spots[0]].set(smallest).at[spots[1]].set(largest)


def cumulative_ranks(count, slope):
    loads = [(1 << 20) // math.isqrt(standing ** slope) + 1 for standing in range(1, count + 1)]
    scale = 1 + sum(loads) // (1 << 30)
    return np.cumsum(np.array([max(1, weight // scale) for weight in loads]))


def ranked_ids(key, extent, count, lean):
    listing = cumulative_ranks(count, lean)
    lot = jax.random.randint(jax.random.fold_in(key, 1), extent, 0, int(listing[count - 1]))
    grade = jnp.searchsorted(jnp.asarray(listing, jnp.int32), lot, side="right")
    return jax.random.permutation(jax.random.fold_in(key, 2), count)[grade].astype(jnp.int32)


def setup_inputs(seed: int = 0) -> dict:
    key_of = jax.random.split(jax.random.key(seed), 6)
    return {
        "hidden_states": draw_hidden_states(jax.random.fold_in(key_of[5], 71), 0),
        "norm_gain": jnp.clip(1.0 + 0.1 * jax.random.normal(key_of[1], (D,), jnp.float32), 0.5, 1.5),
        "head": draw_head(jax.random.fold_in(key_of[5], 71), 0),
        "target_ids": touch_ends(ranked_ids(key_of[3], (TOKENS,), VOCAB, 2), jax.random.fold_in(key_of[3], 3), 0, VOCAB - 1).astype(jnp.int32),
        "lengths": draw_lengths(jax.random.fold_in(key_of[5], 71), 0),
    }


def reference(hidden_states, norm_gain, head, target_ids, lengths):
    feats = hidden_states.astype(jnp.float32)
    scale = lax.rsqrt(lax.optimization_barrier(jnp.mean(feats * feats, axis=-1, keepdims=True)) + 1e-06)
    normed = (feats * scale * norm_gain.astype(jnp.float32)).astype(jnp.bfloat16)
    blocks = normed.reshape(NSEQ, LMAX, D)
    targets = target_ids.reshape(NSEQ, LMAX).astype(jnp.int32)

    def one_block(args):
        block, target = args
        logits = jnp.dot(block, head, preferred_element_type=jnp.float32)
        top = lax.optimization_barrier(jnp.max(logits, axis=-1))
        shifted = jnp.exp(logits - top[:, None])
        total = lax.optimization_barrier(jnp.sum(shifted, axis=-1))
        weighted = lax.optimization_barrier(jnp.sum(shifted * logits, axis=-1))
        picked = jnp.take_along_axis(logits, target[:, None], axis=1)[:, 0]
        return (top, total, weighted, picked)
    top, total, weighted, picked = lax.map(one_block, (blocks, targets))
    log_norm = top + jnp.log(total)
    slots = jnp.arange(LMAX, dtype=jnp.int32)
    live = slots[None, :] < lengths.astype(jnp.int32)[:, None]
    logprob = jnp.where(live, picked - log_norm, jnp.float32(0.0))
    entropy = jnp.where(live, log_norm - weighted / total, jnp.float32(0.0))
    mean_lp = lax.optimization_barrier(jnp.sum(logprob, axis=1)) / lengths.astype(jnp.float32)
    top_live = lax.optimization_barrier(jnp.max(jnp.where(live, top, jnp.float32(-1e+30)), axis=1))
    return (logprob.reshape(-1), entropy.reshape(-1), mean_lp, top_live)
```

```python
import functools

import jax
import jax.numpy as jnp
from jax import lax
from jax.experimental import pallas as pl
from jax.experimental.pallas import tpu as pltpu
from jax.sharding import PartitionSpec as P

AXES = ("req", "tp")
LANES = 128
STATS = 8
VMEM_BYTES = 48 * 1024 * 1024


def ring_place(req, n_req):
    half = n_req // 2
    return jnp.where(req % 2 == 0, req // 2, n_req - 1 - req // 2) if half else req


def ring_req(place, n_req):
    half = n_req // 2
    return jnp.where(place < half, 2 * place, 2 * (n_req - 1 - place) + 1)


def ring_req_py(place, n_req):
    place %= n_req
    return 2 * place if place < n_req // 2 else 2 * (n_req - 1 - place) + 1


def ring_pairs(n_req, n_tp, turn):
    pairs = []
    for place in range(n_req):
        here, there = ring_req_py(place, n_req), ring_req_py(place + turn, n_req)
        pairs += [(here * n_tp + t, there * n_tp + t) for t in range(n_tp)]
    return pairs


def tp_pairs(n_req, n_tp, bit):
    return [(r * n_tp + t, r * n_tp + (t ^ bit)) for r in range(n_req) for t in range(n_tp)]


def block_starts(rows, b_rows):
    g = rows // 2 - b_rows
    return (0, g, rows // 2, rows - g), (g, b_rows, b_rows, g)


def norm_kernel(b_rows, x_ref, gain_ref, xn_ref, acw_ref, bcw_ref, accw_ref, bccw_ref):
    rows = x_ref.shape[0]
    plane = lax.axis_index("tp") // 2
    feats = x_ref[...].astype(jnp.float32)
    scale = lax.rsqrt(jnp.mean(feats * feats, axis=-1, keepdims=True) + 1e-06)
    xn_ref[...] = (feats * scale * gain_ref[...]).astype(jnp.bfloat16)
    starts, sizes = block_starts(rows, b_rows)
    for refs, flip in (((acw_ref, bcw_ref), 0), ((accw_ref, bccw_ref), 1)):
        down = plane != flip
        dests = ((refs[0], 0), (refs[0], sizes[0]), (refs[1], 0))
        for j, (ref, at) in enumerate(dests):
            start = pl.multiple_of(jnp.where(down, starts[3 - j], starts[j]), 16)
            ref[pl.ds(at, sizes[j]), :] = xn_ref[pl.ds(start, sizes[j]), :]


def norm_rows(hidden_half, norm_gain, b_rows):
    rows, d = hidden_half.shape
    a = rows // 2
    shapes = [(rows, d), (a, d), (b_rows, d), (a, d), (b_rows, d)]
    return pl.pallas_call(
        functools.partial(norm_kernel, b_rows),
        out_shape=[jax.ShapeDtypeStruct(s, jnp.bfloat16) for s in shapes],
        compiler_params=pltpu.CompilerParams(vmem_limit_bytes=VMEM_BYTES),
        name="norm",
    )(hidden_half, norm_gain.reshape(1, d))


def piece_segments(part, rows, b_rows):
    return {"all": (0, 1, 2, 3), "a": (0, 1), "b": (2,), "y": (3,)}[part]


def stats_kernel(metas, n_req, b_rows, rows, *refs):
    n = len(metas)
    piece_refs, (w0_ref, w1_ref, tid_ref, out_ref, x_s, l_s, t_s, tc_s) = refs[:n], refs[n:]
    req, tp = lax.axis_index("req"), lax.axis_index("tp")
    n_tp = lax.axis_size("tp")
    plane = tp // 2
    place = ring_place(req, n_req)
    vdev = w0_ref.shape[1]
    total = x_s.shape[0]

    lane = lax.broadcasted_iota(jnp.int32, (1, LANES), 1)
    t_s[:, :] = jnp.zeros_like(t_s)
    t_s[:, : tid_ref.shape[0]] = tid_ref[...].T
    starts, sizes = block_starts(rows, b_rows)
    at = 0
    for (turn, hops, part), ref in zip(metas, piece_refs):
        x_s[pl.ds(at, ref.shape[0]), :] = ref[...]
        source = ring_req((place - turn * hops + n_req) % n_req, n_req)
        down = plane != (0 if turn >= 0 else 1)
        for j in piece_segments(part, rows, b_rows):
            start = starts[j] if part == "all" else jnp.where(down, starts[3 - j], starts[j])
            seg = t_s[pl.ds(pl.multiple_of(start, 16), sizes[j]), :]
            tc_s[pl.ds(at, sizes[j]), :] = jnp.sum(
                jnp.where(lane == source, seg, 0), axis=1, keepdims=True
            )
            at += sizes[j]

    x = x_s[...]
    l_s[:, :vdev] = jnp.dot(x, w0_ref[...], preferred_element_type=jnp.float32)
    l_s[:, vdev:] = jnp.dot(x, w1_ref[...], preferred_element_type=jnp.float32)

    column = lax.broadcasted_iota(jnp.int32, (1, vdev), 1)
    ids0 = column + (req * n_tp + tp) * vdev
    ids1 = column + (req * n_tp + (tp ^ 1)) * vdev
    step = 16

    def body(i, _):
        here = pl.ds(pl.multiple_of(i * step, step), step)
        logits = l_s[here, :]
        target = tc_s[here, :]
        top = jnp.max(logits, axis=1, keepdims=True)
        shifted = jnp.exp(logits - top)
        weight_sum = jnp.sum(shifted, axis=1, keepdims=True)
        weighted = jnp.sum(shifted * logits, axis=1, keepdims=True)
        hit0 = jnp.where(ids0 == target, logits[:, :vdev], 0.0)
        hit1 = jnp.where(ids1 == target, logits[:, vdev:], 0.0)
        picked = jnp.sum(hit0 + hit1, axis=1, keepdims=True)
        out_ref[here, :] = jnp.where(
            lane == 0, top, jnp.where(lane == 1, weight_sum, jnp.where(lane == 2, weighted, picked))
        )
        return 0

    lax.fori_loop(0, total // step, body, 0, unroll=2)


def stats_of(pieces, metas, w0, w1, tids, n_req, b_rows, rows):
    d, vdev = w0.shape
    total = sum(p.shape[0] for p in pieces)
    return pl.pallas_call(
        functools.partial(stats_kernel, metas, n_req, b_rows, rows),
        out_shape=jax.ShapeDtypeStruct((total, LANES), jnp.float32),
        scratch_shapes=[
            pltpu.VMEM((total, d), jnp.bfloat16),
            pltpu.VMEM((total, 2 * vdev), jnp.float32),
            pltpu.VMEM((rows, LANES), jnp.int32),
            pltpu.VMEM((total, 1), jnp.int32),
        ],
        compiler_params=pltpu.CompilerParams(vmem_limit_bytes=VMEM_BYTES),
        cost_estimate=pl.CostEstimate(
            flops=4 * total * d * vdev, bytes_accessed=4 * d * vdev, transcendentals=2 * total * vdev
        ),
        name="stats",
    )(*pieces, w0, w1, tids)


def pack_kernel(metas, n_req, n_tp, b_rows, rows, *refs):
    *stat_refs, out_ref = refs
    req, tp = lax.axis_index("req"), lax.axis_index("tp")
    plane = tp // 2
    place = ring_place(req, n_req)
    starts, sizes = block_starts(rows, b_rows)
    shards = {}
    for meta, ref in zip(metas, stat_refs):
        at = 0
        for turn, hops, part in meta:
            for j in piece_segments(part, rows, b_rows):
                shards.setdefault((turn, hops) if 2 * hops != n_req else (0, hops), []).append(
                    (turn, j, ref[pl.ds(at, sizes[j]), :])
                )
                at += sizes[j]
    for (turn, hops), found in shards.items():
        if turn == 0 and hops:
            up = {j: v for t, j, v in found if t > 0} | {3 - j: v for t, j, v in found if t < 0}
        else:
            up = {j: v for _, j, v in found}
        ordered = jnp.concatenate([up[j] for j in range(4)], axis=0)
        if hops:
            flipped = jnp.concatenate([up[3 - j] for j in range(4)], axis=0)
            down = plane != (0 if turn >= 0 else 1)
            ordered = jnp.where(down, flipped, ordered)
        source = ring_req((place - turn * hops + n_req) % n_req, n_req)
        if turn == 0 and hops:
            source = ring_req((place + hops) % n_req, n_req)
        packed = ordered.T[:STATS, :]
        for t in range(n_tp):
            out_ref[source * n_tp + t] = packed


def pack(stats, metas, n_req, n_tp, b_rows, rows):
    return pl.pallas_call(
        functools.partial(pack_kernel, metas, n_req, n_tp, b_rows, rows),
        out_shape=jax.ShapeDtypeStruct((n_req * n_tp, STATS, rows), jnp.float32),
        compiler_params=pltpu.CompilerParams(vmem_limit_bytes=VMEM_BYTES),
        name="pack",
    )(*stats)


def final_kernel(n_parts, r_ref, len_ref, lp_ref, ent_ref, mean_ref, top_ref):
    rows = r_ref.shape[2]
    length = len_ref[0]
    total = jnp.float32(0.0)
    best = jnp.float32(-1e30)
    for half in range(2):
        mine = [r_ref[2 * k + half] for k in range(n_parts // 2)]
        top = functools.reduce(jnp.maximum, [m[0:1] for m in mine])
        scaled = functools.reduce(jnp.add, [m * jnp.exp(m[0:1] - top) for m in mine])
        picked = functools.reduce(jnp.add, [m[3:4] for m in mine])
        weight_sum, weighted = scaled[1:2], scaled[2:3]
        log_norm = top + jnp.log(weight_sum)
        slot = lax.broadcasted_iota(jnp.int32, (1, rows), 1) + half * rows
        live = slot < length
        logprob = jnp.where(live, picked - log_norm, 0.0)
        lp_ref[half : half + 1, :] = logprob
        ent_ref[half : half + 1, :] = jnp.where(live, log_norm - weighted / weight_sum, 0.0)
        total += jnp.sum(logprob)
        best = jnp.maximum(best, jnp.max(jnp.where(live, top, -1e30)))
    mean_ref[...] = jnp.full((1, 1), total, jnp.float32) / length.astype(jnp.float32)
    top_ref[...] = jnp.full((1, 1), best, jnp.float32)


def finish(received, lengths):
    n_parts, _, rows = received.shape
    outs = pl.pallas_call(
        functools.partial(final_kernel, n_parts),
        out_shape=[jax.ShapeDtypeStruct((2, rows), jnp.float32)] * 2
        + [jax.ShapeDtypeStruct((1, 1), jnp.float32)] * 2,
        in_specs=[
            pl.BlockSpec(memory_space=pltpu.VMEM),
            pl.BlockSpec(memory_space=pltpu.SMEM),
        ],
        name="finish",
    )(received, lengths)
    return tuple(o.reshape(-1) for o in outs)


def per_device(n_req, n_tp, hidden_states, norm_gain, head, target_ids, lengths):
    rows = hidden_states.shape[0] // 2
    b_rows = rows // 4
    core = lax.axis_index("tp") % 2
    cw, ccw = ring_pairs(n_req, n_tp, 1), ring_pairs(n_req, n_tp, -1)
    other_core, other_y = tp_pairs(n_req, n_tp, 1), tp_pairs(n_req, n_tp, 2)

    def send(value, pairs):
        return lax.ppermute(value, AXES, pairs)

    other_head = send(head, other_core)
    hidden_half = lax.dynamic_slice_in_dim(hidden_states, core * rows, rows, 0)
    xn, a_cw, b_cw, a_ccw, b_ccw = norm_rows(hidden_half, norm_gain, b_rows)
    my_targets = lax.dynamic_slice_in_dim(target_ids, core * rows, rows, 0)
    tids = lax.all_to_all(
        jnp.broadcast_to(my_targets[None, :], (n_req, rows)), "req", 0, 0, tiled=True
    )
    metas, stats = [], []

    def work(pieces, meta):
        metas.append(tuple(meta))
        stats.append(
            stats_of(pieces, tuple(meta), head, other_head, tids, n_req, b_rows, rows)
        )

    pieces, meta = [xn], [(0, 0, "all")]
    g = rows // 2 - b_rows
    for hops in range(1, n_req // 2 + 1):
        last = 2 * hops == n_req
        a_cw, a_ccw = send(a_cw, cw), send(a_ccw, ccw)
        if not last:
            b_cw, b_ccw = send(b_cw, cw), send(b_ccw, ccw)
        work(pieces, meta)
        if last:
            pieces, meta = [a_cw, a_ccw], [(1, hops, "a"), (-1, hops, "a")]
        else:
            pieces = [a_cw, b_cw, a_ccw, b_ccw]
            meta = [(1, hops, "a"), (1, hops, "b"), (-1, hops, "a"), (-1, hops, "b")]
        if hops > 1:
            pieces += [y_piece[:g], y_piece[g:]]
            meta += [(1, hops - 1, "y"), (-1, hops - 1, "y")]
        if not last:
            y_piece = send(jnp.concatenate([a_cw[:g], a_ccw[:g]], axis=0), other_y)
    work(pieces, meta)
    packed = pack(stats, metas, n_req, n_tp, b_rows, rows)
    received = lax.all_to_all(packed, AXES, 0, 0, tiled=True)
    return finish(received, lengths)


def solution(mesh):
    n_req, n_tp = mesh.shape["req"], mesh.shape["tp"]
    in_specs = (P("req", None), P(), P(None, ("req", "tp")), P("req"), P("req"))
    out_specs = (P("req"), P("req"), P("req"), P("req"))
    return jax.shard_map(
        functools.partial(per_device, n_req, n_tp),
        mesh=mesh,
        in_specs=in_specs,
        out_specs=out_specs,
        check_vma=False,
    )
```

```python
import functools

import jax
import jax.numpy as jnp
from jax import lax
from jax.experimental import pallas as pl
from jax.experimental.pallas import tpu as pltpu
from jax.sharding import PartitionSpec as P

AXES = ("req", "tp")
LANES = 128
STATS = 8
DIGIT_BITS = 7
VMEM_BYTES = 10 * 1024 * 1024


def ring_place(req, n_req):
    half = n_req // 2
    return jnp.where(req % 2 == 0, req // 2, n_req - 1 - req // 2) if half else req


def ring_req(place, n_req):
    half = n_req // 2
    return jnp.where(place < half, 2 * place, 2 * (n_req - 1 - place) + 1)


def ring_req_py(place, n_req):
    place %= n_req
    return 2 * place if place < n_req // 2 else 2 * (n_req - 1 - place) + 1


def ring_pairs(n_req, n_tp, turn):
    pairs = []
    for place in range(n_req):
        here, there = ring_req_py(place, n_req), ring_req_py(place + turn, n_req)
        pairs += [(here * n_tp + t, there * n_tp + t) for t in range(n_tp)]
    return pairs


def tp_pairs(n_req, n_tp, bit):
    return [(r * n_tp + t, r * n_tp + (t ^ bit)) for r in range(n_req) for t in range(n_tp)]


def block_starts(rows, b_rows):
    g = rows // 2 - b_rows
    return (0, g, rows // 2, rows - g), (g, b_rows, b_rows, g)


def digits(target, first):
    lane = lax.broadcasted_iota(jnp.int32, (1, LANES), 1) - first
    shift = jnp.where(lane == 0, 2 * DIGIT_BITS, jnp.where(lane == 1, DIGIT_BITS, 0))
    digit = (target >> shift) & ((1 << DIGIT_BITS) - 1)
    return jnp.where((lane >= 0) & (lane < 3), digit, 0)


def undigits(ext, first):
    lane = lax.broadcasted_iota(jnp.int32, (1, LANES), 1) - first
    base = float(1 << DIGIT_BITS)
    weight = jnp.where(
        lane == 0, base * base, jnp.where(lane == 1, base, jnp.where(lane == 2, 1.0, 0.0))
    )
    return jnp.sum(ext.astype(jnp.float32) * weight, axis=1, keepdims=True)


def norm_kernel(
    b_rows, x_hbm, gain_hbm, tid_ref, xn_ref, acw_ref, bcw_ref, accw_ref, bccw_ref,
    x_ref, gain_ref, ext_ref, sems,
):
    rows, d = x_ref.shape
    tp = lax.axis_index("tp")
    core, plane = tp % 2, tp // 2
    mine = pl.ds(pl.multiple_of(core * rows, rows), rows)
    get_x = pltpu.make_async_copy(x_hbm.at[mine, :], x_ref, sems.at[0])
    get_gain = pltpu.make_async_copy(gain_hbm, gain_ref, sems.at[1])
    get_x.start()
    get_gain.start()
    target = jnp.where(core == 0, tid_ref[0:1, :], tid_ref[1:2, :])
    target = jnp.broadcast_to(target, (8, rows)).T[:, :1]
    ext = digits(target, 0)
    ext_ref[0] = ext
    ext_ref[1] = digits(target, 3)
    xn_ref[:, d:] = ext.astype(jnp.float32).astype(jnp.bfloat16)
    get_x.wait()
    get_gain.wait()
    feats = x_ref[...].astype(jnp.float32)
    scale = lax.rsqrt(jnp.mean(feats * feats, axis=-1, keepdims=True) + 1e-06)
    xn_ref[:, :d] = (feats * scale * gain_ref[...]).astype(jnp.bfloat16)
    starts, sizes = block_starts(rows, b_rows)
    for a_ref, b_ref, flip in ((acw_ref, bcw_ref, 0), (accw_ref, bccw_ref, 1)):
        down = plane != flip
        place = [
            pl.ds(pl.multiple_of(jnp.where(down, starts[3 - j], starts[j]), 16), sizes[j])
            for j in range(3)
        ]
        at = 0
        for j in range(2):
            here = pl.ds(at, sizes[j])
            a_ref[here, :d] = xn_ref[place[j], :d]
            own = ext_ref[0, place[j], :]
            if at < b_rows:
                part = min(b_rows - at, sizes[j])
                beside = pl.ds(pl.multiple_of(place[2].start + at, 16), part)
                a_ref[pl.ds(at, part), d:] = (
                    (own[:part] + ext_ref[1, beside, :]).astype(jnp.float32).astype(jnp.bfloat16)
                )
                if part < sizes[j]:
                    a_ref[pl.ds(at + part, sizes[j] - part), d:] = (
                        own[part:].astype(jnp.float32).astype(jnp.bfloat16)
                    )
            else:
                a_ref[here, d:] = own.astype(jnp.float32).astype(jnp.bfloat16)
            at += sizes[j]
        b_ref[...] = xn_ref[place[2], :d]


def norm_rows(hidden, norm_gain, target_ids, rows, b_rows):
    d = hidden.shape[1]
    a, wide = rows // 2, d + LANES
    shapes = [(rows, wide), (a, wide), (b_rows, d), (a, wide), (b_rows, d)]
    return pl.pallas_call(
        functools.partial(norm_kernel, b_rows),
        out_shape=[jax.ShapeDtypeStruct(s, jnp.bfloat16) for s in shapes],
        in_specs=[pl.BlockSpec(memory_space=pl.ANY)] * 2 + [pl.BlockSpec(memory_space=pltpu.VMEM)],
        scratch_shapes=[
            pltpu.VMEM((rows, d), jnp.bfloat16),
            pltpu.VMEM((1, d), jnp.float32),
            pltpu.VMEM((2, rows, LANES), jnp.int32),
            pltpu.SemaphoreType.DMA((2,)),
        ],
        compiler_params=pltpu.CompilerParams(vmem_limit_bytes=VMEM_BYTES),
        name="norm",
    )(
        pltpu.with_memory_space_constraint(hidden, pltpu.HBM),
        pltpu.with_memory_space_constraint(norm_gain.reshape(1, d), pltpu.HBM),
        target_ids.reshape(2, rows),
    )


def join_kernel(first_ref, second_ref, out_ref):
    half = out_ref.shape[0] // 2
    out_ref[:half, :] = first_ref[:half, :]
    out_ref[half:, :] = second_ref[:half, :]


def join_heads(first, second, count):
    return pl.pallas_call(
        join_kernel,
        out_shape=jax.ShapeDtypeStruct((2 * count, first.shape[1]), first.dtype),
        compiler_params=pltpu.CompilerParams(vmem_limit_bytes=VMEM_BYTES),
        name="join",
    )(first, second)


def piece_segments(part):
    return {"all": (0, 1, 2, 3), "a": (0, 1), "b": (2,), "y": (3,)}[part]


def stats_kernel(metas, n_req, n_tp, b_rows, rows, earlier, tail, *refs):
    n = len(metas)
    piece_refs, (w0_ref, w1_ref), refs = refs[:n], refs[n : n + 2], refs[n + 2 :]
    if tail:
        stat_refs, (packed_ref, x_s, l_s, t_s, out_ref) = refs[: len(earlier)], refs[len(earlier) :]
    else:
        out_ref, x_s, l_s, t_s = refs
    req, tp = lax.axis_index("req"), lax.axis_index("tp")
    d, vdev = w0_ref.shape
    total = x_s.shape[0]

    lane = lax.broadcasted_iota(jnp.int32, (1, LANES), 1)
    at = 0
    for parts, ref in zip(metas, piece_refs):
        here = pl.ds(at, ref.shape[0])
        x_s[here, :] = ref[:, :d]
        if parts[0][2] == "b":
            t_s[here, :] = undigits(before[: ref.shape[0], d:], 3)
        else:
            t_s[here, :] = undigits(ref[:, d:], 0)
        before = ref
        at += ref.shape[0]

    x = x_s[...]
    l_s[:, :vdev] = jnp.dot(x, w0_ref[...], preferred_element_type=jnp.float32)
    l_s[:, vdev:] = jnp.dot(x, w1_ref[...], preferred_element_type=jnp.float32)

    column = lax.broadcasted_iota(jnp.int32, (1, vdev), 1)
    ids0 = (column + (req * n_tp + tp) * vdev).astype(jnp.float32)
    ids1 = (column + (req * n_tp + (tp ^ 1)) * vdev).astype(jnp.float32)
    step = 16

    def body(i, _):
        here = pl.ds(pl.multiple_of(i * step, step), step)
        logits = l_s[here, :]
        target = t_s[here, :]
        top = jnp.max(logits, axis=1, keepdims=True)
        shifted = jnp.exp(logits - top)
        weight_sum = jnp.sum(shifted, axis=1, keepdims=True)
        weighted = jnp.sum(shifted * logits, axis=1, keepdims=True)
        hit0 = jnp.where(ids0 == target, logits[:, :vdev], 0.0)
        hit1 = jnp.where(ids1 == target, logits[:, vdev:], 0.0)
        picked = jnp.sum(hit0 + hit1, axis=1, keepdims=True)
        out_ref[here, :] = jnp.where(
            lane == 0, top, jnp.where(lane == 1, weight_sum, jnp.where(lane == 2, weighted, picked))
        )
        return 0

    lax.fori_loop(0, total // step, body, 0, unroll=4)
    if tail:
        pack_stats(earlier + (metas,), (*stat_refs, out_ref), packed_ref, n_req, n_tp, b_rows, rows)


def pack_stats(metas, stat_refs, packed_ref, n_req, n_tp, b_rows, rows):
    plane = lax.axis_index("tp") // 2
    place = ring_place(lax.axis_index("req"), n_req)
    starts, sizes = block_starts(rows, b_rows)
    shards = {}
    for pieces, ref in zip(metas, stat_refs):
        at = 0
        for turn, hops, part in (p for parts in pieces for p in parts):
            for j in piece_segments(part):
                shards.setdefault((turn, hops) if 2 * hops != n_req else (0, hops), []).append(
                    (turn, j, ref[pl.ds(at, sizes[j]), :])
                )
                at += sizes[j]
    for (turn, hops), found in shards.items():
        if turn == 0 and hops:
            up = {j: v for t, j, v in found if t > 0} | {3 - j: v for t, j, v in found if t < 0}
        else:
            up = {j: v for _, j, v in found}
        ordered = jnp.concatenate([up[j] for j in range(4)], axis=0)
        if hops:
            flipped = jnp.concatenate([up[3 - j] for j in range(4)], axis=0)
            down = plane != (0 if turn >= 0 else 1)
            ordered = jnp.where(down, flipped, ordered)
        source = ring_req((place - (turn or 1) * hops + n_req) % n_req, n_req)
        packed = ordered.T[:STATS, :]
        for t in range(n_tp):
            packed_ref[source * n_tp + t] = packed


def stats_of(pieces, metas, w0, w1, n_req, n_tp, b_rows, rows, earlier=(), stats=(), tail=False):
    d, vdev = w0.shape
    total = sum(p.shape[0] for p in pieces)
    row_stats = (total, LANES)
    return pl.pallas_call(
        functools.partial(stats_kernel, metas, n_req, n_tp, b_rows, rows, earlier, tail),
        out_shape=jax.ShapeDtypeStruct(
            (n_req * n_tp, STATS, rows) if tail else row_stats, jnp.float32
        ),
        scratch_shapes=[
            pltpu.VMEM((total, d), jnp.bfloat16),
            pltpu.VMEM((total, 2 * vdev), jnp.float32),
            pltpu.VMEM((total, 1), jnp.float32),
        ]
        + [pltpu.VMEM(row_stats, jnp.float32)] * tail,
        compiler_params=pltpu.CompilerParams(vmem_limit_bytes=VMEM_BYTES),
        cost_estimate=pl.CostEstimate(
            flops=4 * total * d * vdev, bytes_accessed=4 * d * vdev, transcendentals=2 * total * vdev
        ),
        name="stats_last" if tail else "stats",
    )(*pieces, w0, w1, *stats)


def final_kernel(n_parts, r_ref, len_ref, lp_ref, ent_ref, mean_ref, top_ref):
    rows = r_ref.shape[2]
    length = len_ref[0]
    total = jnp.float32(0.0)
    best = jnp.float32(-1e30)
    for half in range(2):
        mine = [r_ref[2 * k + half] for k in range(n_parts // 2)]
        top = functools.reduce(jnp.maximum, [m[0:1] for m in mine])
        scaled = functools.reduce(jnp.add, [m * jnp.exp(m[0:1] - top) for m in mine])
        picked = functools.reduce(jnp.add, [m[3:4] for m in mine])
        weight_sum, weighted = scaled[1:2], scaled[2:3]
        log_norm = top + jnp.log(weight_sum)
        slot = lax.broadcasted_iota(jnp.int32, (1, rows), 1) + half * rows
        live = slot < length
        logprob = jnp.where(live, picked - log_norm, 0.0)
        lp_ref[half : half + 1, :] = logprob
        ent_ref[half : half + 1, :] = jnp.where(live, log_norm - weighted / weight_sum, 0.0)
        total += jnp.sum(logprob)
        best = jnp.maximum(best, jnp.max(jnp.where(live, top, -1e30)))
    mean_ref[...] = jnp.full((1, 1), total, jnp.float32) / length.astype(jnp.float32)
    top_ref[...] = jnp.full((1, 1), best, jnp.float32)


def finish(received, lengths):
    n_parts, _, rows = received.shape
    outs = pl.pallas_call(
        functools.partial(final_kernel, n_parts),
        out_shape=[jax.ShapeDtypeStruct((2, rows), jnp.float32)] * 2
        + [jax.ShapeDtypeStruct((1, 1), jnp.float32)] * 2,
        in_specs=[
            pl.BlockSpec(memory_space=pltpu.VMEM),
            pl.BlockSpec(memory_space=pltpu.SMEM),
        ],
        compiler_params=pltpu.CompilerParams(vmem_limit_bytes=VMEM_BYTES),
        name="finish",
    )(received, lengths)
    return tuple(o.reshape(-1) for o in outs)


def per_device(n_req, n_tp, hidden_states, norm_gain, head, target_ids, lengths):
    rows = hidden_states.shape[0] // 2
    b_rows = rows // 4
    cw, ccw = ring_pairs(n_req, n_tp, 1), ring_pairs(n_req, n_tp, -1)
    other_core, other_y = tp_pairs(n_req, n_tp, 1), tp_pairs(n_req, n_tp, 2)

    def send(value, pairs):
        return lax.ppermute(value, AXES, pairs)

    other_head = send(head, other_core)
    xn, a_cw, b_cw, a_ccw, b_ccw = norm_rows(hidden_states, norm_gain, target_ids, rows, b_rows)
    sizes = (n_req, n_tp, b_rows, rows)
    g = rows // 2 - b_rows
    meta = (((0, 0, "all"),),)
    metas = [meta]
    stats = [stats_of([xn], meta, head, other_head, *sizes)]
    y_piece = None
    for hops in range(1, n_req // 2 + 1):
        last = 2 * hops == n_req
        a_cw, a_ccw = send(a_cw, cw), send(a_ccw, ccw)
        if not last:
            b_cw, b_ccw = send(b_cw, cw), send(b_ccw, ccw)
        if hops > 1:
            y_next = send(y_message, other_y)
            stats.append(stats_of(pieces, meta, head, other_head, *sizes))
            metas.append(meta)
        a_cw, a_ccw, stats[-1] = lax.optimization_barrier((a_cw, a_ccw, stats[-1]))
        if last:
            pieces, meta = [a_cw, a_ccw], [((1, hops, "a"),), ((-1, hops, "a"),)]
        else:
            y_message = join_heads(a_cw, a_ccw, g)
            pieces = [a_cw, b_cw, a_ccw, b_ccw]
            meta = [((1, hops, "a"),), ((1, hops, "b"),), ((-1, hops, "a"),), ((-1, hops, "b"),)]
        if hops > 1:
            pieces.append(y_next)
            meta.append(((1, hops - 1, "y"), (-1, hops - 1, "y")))
        meta = tuple(meta)
    packed = stats_of(
        pieces, meta, head, other_head, *sizes, earlier=tuple(metas), stats=stats, tail=True
    )
    received = lax.all_to_all(packed, AXES, 0, 0, tiled=True)
    return finish(received, lengths)


def solution(mesh):
    n_req, n_tp = mesh.shape["req"], mesh.shape["tp"]
    in_specs = (P("req", None), P(), P(None, ("req", "tp")), P("req"), P("req"))
    out_specs = (P("req"), P("req"), P("req"), P("req"))
    return jax.shard_map(
        functools.partial(per_device, n_req, n_tp),
        mesh=mesh,
        in_specs=in_specs,
        out_specs=out_specs,
        check_vma=False,
    )
```

```python
import functools

import jax
import jax.numpy as jnp
from jax import lax
from jax.experimental import pallas as pl
from jax.experimental.pallas import tpu as pltpu
from jax.sharding import PartitionSpec as P

AXES = ("req", "tp")
LANES = 128
STATS = 8
DIGIT_BITS = 7
VMEM_BYTES = 10 * 1024 * 1024


def ring_place(req, n_req):
    half = n_req // 2
    return jnp.where(req % 2 == 0, req // 2, n_req - 1 - req // 2) if half else req


def ring_req(place, n_req):
    half = n_req // 2
    return jnp.where(place < half, 2 * place, 2 * (n_req - 1 - place) + 1)


def ring_req_py(place, n_req):
    place %= n_req
    return 2 * place if place < n_req // 2 else 2 * (n_req - 1 - place) + 1


def ring_pairs(n_req, n_tp, turn):
    pairs = []
    for place in range(n_req):
        here, there = ring_req_py(place, n_req), ring_req_py(place + turn, n_req)
        pairs += [(here * n_tp + t, there * n_tp + t) for t in range(n_tp)]
    return pairs


def tp_pairs(n_req, n_tp, bit):
    return [(r * n_tp + t, r * n_tp + (t ^ bit)) for r in range(n_req) for t in range(n_tp)]


def block_starts(rows, b_rows):
    g = rows // 2 - b_rows
    return (0, g, rows // 2, rows - g), (g, b_rows, b_rows, g)


def digits(target):
    lane = lax.broadcasted_iota(jnp.int32, (1, LANES), 1)
    shift = jnp.where(lane == 0, 2 * DIGIT_BITS, jnp.where(lane == 1, DIGIT_BITS, 0))
    digit = (target >> shift) & ((1 << DIGIT_BITS) - 1)
    return jnp.where(lane < 3, digit, 0).astype(jnp.float32).astype(jnp.bfloat16)


def undigits(ext):
    lane = lax.broadcasted_iota(jnp.int32, (1, LANES), 1)
    base = float(1 << DIGIT_BITS)
    weight = jnp.where(
        lane == 0, base * base, jnp.where(lane == 1, base, jnp.where(lane == 2, 1.0, 0.0))
    )
    return jnp.sum(ext.astype(jnp.float32) * weight, axis=1, keepdims=True)


def norm_kernel(
    b_rows, x_hbm, gain_hbm, tid_hbm, xn_ref, cw_ref, ccw_ref, x_ref, gain_ref, tid_ref, sems
):
    rows, d = x_ref.shape
    tp = lax.axis_index("tp")
    core, plane = tp % 2, tp // 2
    mine = pl.ds(pl.multiple_of(core * rows, rows), rows)
    get_x = pltpu.make_async_copy(x_hbm.at[mine, :], x_ref, sems.at[0])
    get_gain = pltpu.make_async_copy(gain_hbm, gain_ref, sems.at[1])
    get_tid = pltpu.make_async_copy(tid_hbm, tid_ref, sems.at[2])
    get_x.start()
    get_gain.start()
    get_tid.start()
    get_tid.wait()
    target = jnp.where(core == 0, tid_ref[0:1, :], tid_ref[1:2, :])
    xn_ref[:, d:] = digits(jnp.broadcast_to(target, (8, rows)).T[:, :1])
    get_gain.wait()
    get_x.wait()
    feats = x_ref[...].astype(jnp.float32)
    scale = lax.rsqrt(jnp.mean(feats * feats, axis=-1, keepdims=True) + 1e-06)
    xn_ref[:, :d] = (feats * scale * gain_ref[...]).astype(jnp.bfloat16)
    starts, sizes = block_starts(rows, b_rows)
    for ref, flip in ((cw_ref, 0), (ccw_ref, 1)):
        down = plane != flip
        at = 0
        for j in range(3):
            start = pl.multiple_of(jnp.where(down, starts[3 - j], starts[j]), 16)
            ref[pl.ds(at, sizes[j]), :] = xn_ref[pl.ds(start, sizes[j]), :]
            at += sizes[j]


def norm_rows(hidden, norm_gain, target_ids, rows, b_rows):
    d = hidden.shape[1]
    wide = d + LANES
    shapes = [(rows, wide), (rows // 2 + b_rows, wide), (rows // 2 + b_rows, wide)]
    hbm_operands = (hidden, norm_gain.reshape(1, d), target_ids.reshape(2, rows))
    return pl.pallas_call(
        functools.partial(norm_kernel, b_rows),
        out_shape=[jax.ShapeDtypeStruct(s, jnp.bfloat16) for s in shapes],
        in_specs=[pl.BlockSpec(memory_space=pl.ANY)] * 3,
        scratch_shapes=[
            pltpu.VMEM((rows, d), jnp.bfloat16),
            pltpu.VMEM((1, d), jnp.float32),
            pltpu.VMEM((2, rows), jnp.int32),
            pltpu.SemaphoreType.DMA((3,)),
        ],
        compiler_params=pltpu.CompilerParams(vmem_limit_bytes=VMEM_BYTES),
        name="norm",
    )(*(pltpu.with_memory_space_constraint(v, pltpu.HBM) for v in hbm_operands))


def join_kernel(first_ref, second_ref, joined_ref, *head_refs):
    half = joined_ref.shape[0] // 2
    joined_ref[:half, :] = first_ref[:half, :]
    joined_ref[half:, :] = second_ref[:half, :]
    for ref, head_ref in zip((first_ref, second_ref), head_refs):
        head_ref[...] = ref[: head_ref.shape[0], :]


def join_heads(first, second, count, head_count=0):
    wide = first.shape[1]
    shapes = [(2 * count, wide)] + [(head_count, wide)] * (2 if head_count else 0)
    return pl.pallas_call(
        join_kernel,
        out_shape=[jax.ShapeDtypeStruct(s, first.dtype) for s in shapes],
        compiler_params=pltpu.CompilerParams(vmem_limit_bytes=VMEM_BYTES),
        name="join",
    )(first, second)


def piece_segments(part):
    return {"all": (0, 1, 2, 3), "most": (0, 1, 2), "half": (0, 1), "y": (3,)}[part]


def stats_kernel(metas, n_req, n_tp, b_rows, rows, earlier, tail, *refs):
    n = len(metas)
    piece_refs, (w0_ref, w1_ref), refs = refs[:n], refs[n : n + 2], refs[n + 2 :]
    if tail:
        stat_refs, (packed_ref, x_s, l_s, t_s, out_ref) = refs[: len(earlier)], refs[len(earlier) :]
    else:
        out_ref, x_s, l_s, t_s = refs
    req, tp = lax.axis_index("req"), lax.axis_index("tp")
    d, vdev = w0_ref.shape
    total = x_s.shape[0]

    lane = lax.broadcasted_iota(jnp.int32, (1, LANES), 1)
    at = 0
    for parts, ref in zip(metas, piece_refs):
        here = pl.ds(at, ref.shape[0])
        x_s[here, :] = ref[:, :d]
        t_s[here, :] = undigits(ref[:, d:])
        at += ref.shape[0]

    x = x_s[...]
    l_s[:, :vdev] = jnp.dot(x, w0_ref[...], preferred_element_type=jnp.float32)
    l_s[:, vdev:] = jnp.dot(x, w1_ref[...], preferred_element_type=jnp.float32)

    column = lax.broadcasted_iota(jnp.int32, (1, vdev), 1)
    ids0 = (column + (req * n_tp + tp) * vdev).astype(jnp.float32)
    ids1 = (column + (req * n_tp + (tp ^ 1)) * vdev).astype(jnp.float32)
    step = 16

    def body(i, _):
        here = pl.ds(pl.multiple_of(i * step, step), step)
        logits = l_s[here, :]
        target = t_s[here, :]
        top = jnp.max(logits, axis=1, keepdims=True)
        shifted = jnp.exp(logits - top)
        weight_sum = jnp.sum(shifted, axis=1, keepdims=True)
        weighted = jnp.sum(shifted * logits, axis=1, keepdims=True)
        hit0 = jnp.where(ids0 == target, logits[:, :vdev], 0.0)
        hit1 = jnp.where(ids1 == target, logits[:, vdev:], 0.0)
        picked = jnp.sum(hit0 + hit1, axis=1, keepdims=True)
        out_ref[here, :] = jnp.where(
            lane == 0, top, jnp.where(lane == 1, weight_sum, jnp.where(lane == 2, weighted, picked))
        )
        return 0

    lax.fori_loop(0, total // step, body, 0, unroll=4)
    if tail:
        pack_stats(earlier + (metas,), (*stat_refs, out_ref), packed_ref, n_req, n_tp, b_rows, rows)


def pack_stats(metas, stat_refs, packed_ref, n_req, n_tp, b_rows, rows):
    plane = lax.axis_index("tp") // 2
    place = ring_place(lax.axis_index("req"), n_req)
    starts, sizes = block_starts(rows, b_rows)
    shards = {}
    for pieces, ref in zip(metas, stat_refs):
        at = 0
        for turn, hops, part in (p for parts in pieces for p in parts):
            for j in piece_segments(part):
                shards.setdefault((turn, hops) if 2 * hops != n_req else (0, hops), []).append(
                    (turn, j, ref[pl.ds(at, sizes[j]), :])
                )
                at += sizes[j]
    for (turn, hops), found in shards.items():
        if turn == 0 and hops:
            up = {j: v for t, j, v in found if t > 0} | {3 - j: v for t, j, v in found if t < 0}
        else:
            up = {j: v for _, j, v in found}
        ordered = jnp.concatenate([up[j] for j in range(4)], axis=0)
        if hops:
            flipped = jnp.concatenate([up[3 - j] for j in range(4)], axis=0)
            down = plane != (0 if turn >= 0 else 1)
            ordered = jnp.where(down, flipped, ordered)
        source = ring_req((place - (turn or 1) * hops + n_req) % n_req, n_req)
        packed = ordered.T[:STATS, :]
        for t in range(n_tp):
            packed_ref[source * n_tp + t] = packed


def stats_of(pieces, metas, w0, w1, n_req, n_tp, b_rows, rows, earlier=(), stats=(), tail=False):
    d, vdev = w0.shape
    total = sum(p.shape[0] for p in pieces)
    row_stats = (total, LANES)
    return pl.pallas_call(
        functools.partial(stats_kernel, metas, n_req, n_tp, b_rows, rows, earlier, tail),
        out_shape=jax.ShapeDtypeStruct(
            (n_req * n_tp, STATS, rows) if tail else row_stats, jnp.float32
        ),
        scratch_shapes=[
            pltpu.VMEM((total, d), jnp.bfloat16),
            pltpu.VMEM((total, 2 * vdev), jnp.float32),
            pltpu.VMEM((total, 1), jnp.float32),
        ]
        + [pltpu.VMEM(row_stats, jnp.float32)] * tail,
        compiler_params=pltpu.CompilerParams(vmem_limit_bytes=VMEM_BYTES),
        cost_estimate=pl.CostEstimate(
            flops=4 * total * d * vdev, bytes_accessed=4 * d * vdev, transcendentals=2 * total * vdev
        ),
        name="stats_last" if tail else "stats",
    )(*pieces, w0, w1, *stats)


def final_kernel(n_parts, r_ref, len_ref, lp_ref, ent_ref, mean_ref, top_ref):
    rows = r_ref.shape[2]
    length = len_ref[0]
    total = jnp.float32(0.0)
    best = jnp.float32(-1e30)
    for half in range(2):
        mine = [r_ref[2 * k + half] for k in range(n_parts // 2)]
        top = functools.reduce(jnp.maximum, [m[0:1] for m in mine])
        scaled = functools.reduce(jnp.add, [m * jnp.exp(m[0:1] - top) for m in mine])
        picked = functools.reduce(jnp.add, [m[3:4] for m in mine])
        weight_sum, weighted = scaled[1:2], scaled[2:3]
        log_norm = top + jnp.log(weight_sum)
        slot = lax.broadcasted_iota(jnp.int32, (1, rows), 1) + half * rows
        live = slot < length
        logprob = jnp.where(live, picked - log_norm, 0.0)
        lp_ref[half : half + 1, :] = logprob
        ent_ref[half : half + 1, :] = jnp.where(live, log_norm - weighted / weight_sum, 0.0)
        total += jnp.sum(logprob)
        best = jnp.maximum(best, jnp.max(jnp.where(live, top, -1e30)))
    mean_ref[...] = jnp.full((1, 1), total, jnp.float32) / length.astype(jnp.float32)
    top_ref[...] = jnp.full((1, 1), best, jnp.float32)


def finish(received, lengths):
    n_parts, _, rows = received.shape
    outs = pl.pallas_call(
        functools.partial(final_kernel, n_parts),
        out_shape=[jax.ShapeDtypeStruct((2, rows), jnp.float32)] * 2
        + [jax.ShapeDtypeStruct((1, 1), jnp.float32)] * 2,
        in_specs=[
            pl.BlockSpec(memory_space=pltpu.VMEM),
            pl.BlockSpec(memory_space=pltpu.SMEM),
        ],
        compiler_params=pltpu.CompilerParams(vmem_limit_bytes=VMEM_BYTES),
        name="finish",
    )(received, lengths)
    return tuple(o.reshape(-1) for o in outs)


def per_device(n_req, n_tp, hidden_states, norm_gain, head, target_ids, lengths):
    rows = hidden_states.shape[0] // 2
    b_rows = rows // 4
    cw_pairs, ccw_pairs = ring_pairs(n_req, n_tp, 1), ring_pairs(n_req, n_tp, -1)
    other_core, other_y = tp_pairs(n_req, n_tp, 1), tp_pairs(n_req, n_tp, 2)

    def send(value, pairs):
        return lax.ppermute(value, AXES, pairs)

    other_head = send(head, other_core)
    xn, to_cw, to_ccw = norm_rows(hidden_states, norm_gain, target_ids, rows, b_rows)
    sizes = (n_req, n_tp, b_rows, rows)
    g = rows // 2 - b_rows
    meta = (((0, 0, "all"),),)
    metas = [meta]
    stats = [stats_of([xn], meta, head, other_head, *sizes)]
    for hops in range(1, n_req // 2 + 1):
        last = 2 * hops == n_req
        cw, ccw = send(to_cw, cw_pairs), send(to_ccw, ccw_pairs)
        if hops > 1:
            y_next = send(y_message, other_y)
            stats.append(stats_of(pieces, meta, head, other_head, *sizes))
            metas.append(meta)
        cw, ccw, stats[-1] = lax.optimization_barrier((cw, ccw, stats[-1]))
        part = "half" if last else "most"
        pieces, meta = [cw, ccw], [((1, hops, part),), ((-1, hops, part),)]
        if not last:
            y_message, *heads = join_heads(cw, ccw, g, rows // 2 if 2 * hops + 2 == n_req else 0)
            to_cw, to_ccw = heads or (cw, ccw)
        if hops > 1:
            pieces.append(y_next)
            meta.append(((1, hops - 1, "y"), (-1, hops - 1, "y")))
        meta = tuple(meta)
    packed = stats_of(
        pieces, meta, head, other_head, *sizes, earlier=tuple(metas), stats=stats, tail=True
    )
    received = lax.all_to_all(packed, AXES, 0, 0, tiled=True)
    return finish(received, lengths)


def solution(mesh):
    n_req, n_tp = mesh.shape["req"], mesh.shape["tp"]
    in_specs = (P("req", None), P(), P(None, ("req", "tp")), P("req"), P("req"))
    out_specs = (P("req"), P("req"), P("req"), P("req"))
    return jax.shard_map(
        functools.partial(per_device, n_req, n_tp),
        mesh=mesh,
        in_specs=in_specs,
        out_specs=out_specs,
        check_vma=False,
    )
```

```python
import functools

import jax
import jax.numpy as jnp
from jax import lax
from jax.experimental import pallas as pl
from jax.experimental.pallas import tpu as pltpu
from jax.sharding import PartitionSpec as P

AXES = ("req", "tp")
LANES = 128
STATS = 8
DIGIT_BITS = 7
VMEM_BYTES = 10 * 1024 * 1024


def ring_place(req, n_req):
    half = n_req // 2
    return jnp.where(req % 2 == 0, req // 2, n_req - 1 - req // 2) if half else req


def ring_req(place, n_req):
    half = n_req // 2
    return jnp.where(place < half, 2 * place, 2 * (n_req - 1 - place) + 1)


def ring_req_py(place, n_req):
    place %= n_req
    return 2 * place if place < n_req // 2 else 2 * (n_req - 1 - place) + 1


def ring_pairs(n_req, n_tp, turn):
    pairs = []
    for place in range(n_req):
        here, there = ring_req_py(place, n_req), ring_req_py(place + turn, n_req)
        pairs += [(here * n_tp + t, there * n_tp + t) for t in range(n_tp)]
    return pairs


def tp_pairs(n_req, n_tp, bit):
    return [(r * n_tp + t, r * n_tp + (t ^ bit)) for r in range(n_req) for t in range(n_tp)]


def segments(rows):
    e = rows // 8
    return (0, 2 * e, 3 * e, 4 * e, 5 * e, 6 * e), (2 * e, e, e, e, e, 2 * e)


PARTS = {
    "all": (0, 1, 2, 3, 4, 5),
    "most": (0, 1, 2, 3),
    "half": (0, 1, 2),
    "y": (5, 4),
    "y_last": (5,),
    "c": (4,),
}


def part_rows(part, rows):
    return sum(segments(rows)[1][j] for j in PARTS[part])


def digits(target):
    lane = lax.broadcasted_iota(jnp.int32, (1, LANES), 1)
    shift = jnp.where(lane == 0, 2 * DIGIT_BITS, jnp.where(lane == 1, DIGIT_BITS, 0))
    digit = (target >> shift) & ((1 << DIGIT_BITS) - 1)
    return jnp.where(lane < 3, digit, 0).astype(jnp.float32).astype(jnp.bfloat16)


def undigits(ext):
    lane = lax.broadcasted_iota(jnp.int32, (1, LANES), 1)
    base = float(1 << DIGIT_BITS)
    weight = jnp.where(
        lane == 0, base * base, jnp.where(lane == 1, base, jnp.where(lane == 2, 1.0, 0.0))
    )
    return jnp.sum(ext.astype(jnp.float32) * weight, axis=1, keepdims=True)


def norm_kernel(x_hbm, gain_hbm, tid_hbm, xn_ref, cw_ref, ccw_ref, x_ref, gain_ref, tid_ref, sems):
    rows, d = x_ref.shape
    tp = lax.axis_index("tp")
    core, plane = tp % 2, tp // 2
    mine = pl.ds(pl.multiple_of(core * rows, rows), rows)
    get_x = pltpu.make_async_copy(x_hbm.at[mine, :], x_ref, sems.at[0])
    get_gain = pltpu.make_async_copy(gain_hbm, gain_ref, sems.at[1])
    get_tid = pltpu.make_async_copy(tid_hbm, tid_ref, sems.at[2])
    get_x.start()
    get_gain.start()
    get_tid.start()
    get_tid.wait()
    target = jnp.where(core == 0, tid_ref[0:1, :], tid_ref[1:2, :])
    xn_ref[:, d:] = digits(jnp.broadcast_to(target, (8, rows)).T[:, :1])
    get_gain.wait()
    get_x.wait()
    feats = x_ref[...].astype(jnp.float32)
    scale = lax.rsqrt(jnp.mean(feats * feats, axis=-1, keepdims=True) + 1e-06)
    xn_ref[:, :d] = (feats * scale * gain_ref[...]).astype(jnp.bfloat16)
    starts, sizes = segments(rows)
    for ref, flip in ((cw_ref, 0), (ccw_ref, 1)):
        down = plane != flip
        at = 0
        for j in PARTS["most"]:
            start = pl.multiple_of(jnp.where(down, starts[5 - j], starts[j]), 16)
            ref[pl.ds(at, sizes[j]), :] = xn_ref[pl.ds(start, sizes[j]), :]
            at += sizes[j]


def norm_rows(hidden, norm_gain, target_ids, rows):
    d = hidden.shape[1]
    wide = d + LANES
    message = (part_rows("most", rows), wide)
    shapes = [(rows, wide), message, message]
    hbm_operands = (hidden, norm_gain.reshape(1, d), target_ids.reshape(2, rows))
    return pl.pallas_call(
        norm_kernel,
        out_shape=[jax.ShapeDtypeStruct(s, jnp.bfloat16) for s in shapes],
        in_specs=[pl.BlockSpec(memory_space=pl.ANY)] * 3,
        scratch_shapes=[
            pltpu.VMEM((rows, d), jnp.bfloat16),
            pltpu.VMEM((1, d), jnp.float32),
            pltpu.VMEM((2, rows), jnp.int32),
            pltpu.SemaphoreType.DMA((3,)),
        ],
        compiler_params=pltpu.CompilerParams(vmem_limit_bytes=VMEM_BYTES),
        name="norm",
    )(*(pltpu.with_memory_space_constraint(v, pltpu.HBM) for v in hbm_operands))


def cut_kernel(plan, n_in, *refs):
    for out_ref, pieces in zip(refs[n_in:], plan):
        to = 0
        for k, at, count in pieces:
            out_ref[pl.ds(to, count), :] = refs[k][pl.ds(at, count), :]
            to += count


def cut(arrays, plan):
    wide = arrays[0].shape[1]
    return pl.pallas_call(
        functools.partial(cut_kernel, plan, len(arrays)),
        out_shape=[
            jax.ShapeDtypeStruct((sum(count for _, _, count in pieces), wide), arrays[0].dtype)
            for pieces in plan
        ],
        compiler_params=pltpu.CompilerParams(vmem_limit_bytes=VMEM_BYTES),
        name="cut",
    )(*arrays)


def stats_kernel(metas, n_req, n_tp, rows, earlier, tail, *refs):
    n = len(metas)
    piece_refs, (w0_ref, w1_ref), refs = refs[:n], refs[n : n + 2], refs[n + 2 :]
    if tail:
        stat_refs, (packed_ref, x_s, l_s, t_s, out_ref) = refs[: len(earlier)], refs[len(earlier) :]
    else:
        out_ref, x_s, l_s, t_s = refs
    req, tp = lax.axis_index("req"), lax.axis_index("tp")
    d, vdev = w0_ref.shape
    total = x_s.shape[0]

    lane = lax.broadcasted_iota(jnp.int32, (1, LANES), 1)
    at = 0
    for parts, ref in zip(metas, piece_refs):
        here = pl.ds(at, ref.shape[0])
        x_s[here, :] = ref[:, :d]
        t_s[here, :] = undigits(ref[:, d:])
        at += ref.shape[0]

    x = x_s[...]
    l_s[:, :vdev] = jnp.dot(x, w0_ref[...], preferred_element_type=jnp.float32)
    l_s[:, vdev:] = jnp.dot(x, w1_ref[...], preferred_element_type=jnp.float32)

    column = lax.broadcasted_iota(jnp.int32, (1, vdev), 1)
    ids0 = (column + (req * n_tp + tp) * vdev).astype(jnp.float32)
    ids1 = (column + (req * n_tp + (tp ^ 1)) * vdev).astype(jnp.float32)
    step = 16

    def body(i, _):
        here = pl.ds(pl.multiple_of(i * step, step), step)
        logits = l_s[here, :]
        target = t_s[here, :]
        top = jnp.max(logits, axis=1, keepdims=True)
        shifted = jnp.exp(logits - top)
        weight_sum = jnp.sum(shifted, axis=1, keepdims=True)
        weighted = jnp.sum(shifted * logits, axis=1, keepdims=True)
        hit0 = jnp.where(ids0 == target, logits[:, :vdev], 0.0)
        hit1 = jnp.where(ids1 == target, logits[:, vdev:], 0.0)
        picked = jnp.sum(hit0 + hit1, axis=1, keepdims=True)
        out_ref[here, :] = jnp.where(
            lane == 0, top, jnp.where(lane == 1, weight_sum, jnp.where(lane == 2, weighted, picked))
        )
        return 0

    lax.fori_loop(0, total // step, body, 0, unroll=4)
    if tail:
        pack_stats(earlier + (metas,), (*stat_refs, out_ref), packed_ref, n_req, n_tp, rows)


def pack_stats(metas, stat_refs, packed_ref, n_req, n_tp, rows):
    plane = lax.axis_index("tp") // 2
    place = ring_place(lax.axis_index("req"), n_req)
    _, sizes = segments(rows)
    shards = {}
    for pieces, ref in zip(metas, stat_refs):
        at = 0
        for turn, hops, part in (p for parts in pieces for p in parts):
            for j in PARTS[part]:
                shards.setdefault((turn, hops) if 2 * hops != n_req else (0, hops), []).append(
                    (turn, j, ref[pl.ds(at, sizes[j]), :])
                )
                at += sizes[j]
    for (turn, hops), found in shards.items():
        if turn == 0 and hops:
            up = {j if t > 0 else 5 - j: v for t, j, v in found}
        else:
            up = {j: v for _, j, v in found}
        ordered = jnp.concatenate([up[j] for j in range(6)], axis=0)
        if hops:
            flipped = jnp.concatenate([up[5 - j] for j in range(6)], axis=0)
            down = plane != (0 if turn >= 0 else 1)
            ordered = jnp.where(down, flipped, ordered)
        source = ring_req((place - (turn or 1) * hops + n_req) % n_req, n_req)
        packed = ordered.T[:STATS, :]
        for t in range(n_tp):
            packed_ref[source * n_tp + t] = packed


def stats_of(pieces, metas, w0, w1, n_req, n_tp, rows, earlier=(), stats=(), tail=False):
    d, vdev = w0.shape
    total = sum(p.shape[0] for p in pieces)
    row_stats = (total, LANES)
    return pl.pallas_call(
        functools.partial(stats_kernel, metas, n_req, n_tp, rows, earlier, tail),
        out_shape=jax.ShapeDtypeStruct(
            (n_req * n_tp, STATS, rows) if tail else row_stats, jnp.float32
        ),
        scratch_shapes=[
            pltpu.VMEM((total, d), jnp.bfloat16),
            pltpu.VMEM((total, 2 * vdev), jnp.float32),
            pltpu.VMEM((total, 1), jnp.float32),
        ]
        + [pltpu.VMEM(row_stats, jnp.float32)] * tail,
        compiler_params=pltpu.CompilerParams(vmem_limit_bytes=VMEM_BYTES),
        cost_estimate=pl.CostEstimate(
            flops=4 * total * d * vdev, bytes_accessed=4 * d * vdev, transcendentals=2 * total * vdev
        ),
        name="stats_last" if tail else "stats",
    )(*pieces, w0, w1, *stats)


def final_kernel(n_parts, r_ref, len_ref, lp_ref, ent_ref, mean_ref, top_ref):
    rows = r_ref.shape[2]
    length = len_ref[0]
    total = jnp.float32(0.0)
    best = jnp.float32(-1e30)
    for half in range(2):
        mine = [r_ref[2 * k + half] for k in range(n_parts // 2)]
        top = functools.reduce(jnp.maximum, [m[0:1] for m in mine])
        scaled = functools.reduce(jnp.add, [m * jnp.exp(m[0:1] - top) for m in mine])
        picked = functools.reduce(jnp.add, [m[3:4] for m in mine])
        weight_sum, weighted = scaled[1:2], scaled[2:3]
        log_norm = top + jnp.log(weight_sum)
        slot = lax.broadcasted_iota(jnp.int32, (1, rows), 1) + half * rows
        live = slot < length
        logprob = jnp.where(live, picked - log_norm, 0.0)
        lp_ref[half : half + 1, :] = logprob
        ent_ref[half : half + 1, :] = jnp.where(live, log_norm - weighted / weight_sum, 0.0)
        total += jnp.sum(logprob)
        best = jnp.maximum(best, jnp.max(jnp.where(live, top, -1e30)))
    mean_ref[...] = jnp.full((1, 1), total, jnp.float32) / length.astype(jnp.float32)
    top_ref[...] = jnp.full((1, 1), best, jnp.float32)


def finish(received, lengths):
    n_parts, _, rows = received.shape
    outs = pl.pallas_call(
        functools.partial(final_kernel, n_parts),
        out_shape=[jax.ShapeDtypeStruct((2, rows), jnp.float32)] * 2
        + [jax.ShapeDtypeStruct((1, 1), jnp.float32)] * 2,
        in_specs=[
            pl.BlockSpec(memory_space=pltpu.VMEM),
            pl.BlockSpec(memory_space=pltpu.SMEM),
        ],
        compiler_params=pltpu.CompilerParams(vmem_limit_bytes=VMEM_BYTES),
        name="finish",
    )(received, lengths)
    return tuple(o.reshape(-1) for o in outs)


def per_device(n_req, n_tp, hidden_states, norm_gain, head, target_ids, lengths):
    rows = hidden_states.shape[0] // 2
    cw_pairs, ccw_pairs = ring_pairs(n_req, n_tp, 1), ring_pairs(n_req, n_tp, -1)
    other_core, other_y = tp_pairs(n_req, n_tp, 1), tp_pairs(n_req, n_tp, 2)
    sizes = (n_req, n_tp, rows)
    y_rows, c_rows, half = (part_rows(part, rows) for part in ("y", "c", "half"))
    y_last_rows = part_rows("y_last", rows)
    metas, stats = [], []

    def send(value, pairs):
        return lax.ppermute(value, AXES, pairs)

    def work(items):
        pieces, meta = zip(*items)
        stats.append(stats_of(pieces, meta, head, other_head, *sizes))
        metas.append(meta)

    def after(value):
        value, stats[-1] = lax.optimization_barrier((value, stats[-1]))
        return value

    xn, to_cw, to_ccw = norm_rows(hidden_states, norm_gain, target_ids, rows)
    swapped, xn = lax.optimization_barrier((head, xn))
    other_head = send(swapped, other_core)
    items = [(xn, ((0, 0, "all"),))]
    for hops in range(1, n_req // 2):
        next_to_last = 2 * hops + 2 == n_req
        cw, ccw = send(to_cw, cw_pairs), send(to_ccw, ccw_pairs)
        if hops > 1:
            y_next = send(y_message, other_y)
        work(items)
        cw, ccw = after(cw), after(ccw)
        items = [(cw, ((1, hops, "most"),)), (ccw, ((-1, hops, "most"),))]
        if hops > 1:
            items.append((y_next, ((1, hops - 1, "y"), (-1, hops - 1, "y"))))
        if next_to_last:
            (to_cw,), (to_ccw,) = cut((cw,), [[(0, 0, half)]]), cut((ccw,), [[(0, 0, half)]])
        else:
            to_cw, to_ccw = cw, ccw
        count = y_last_rows if next_to_last else y_rows
        (y_message,) = cut((cw, ccw), [[(0, 0, count), (1, 0, count)]])
    hops = n_req // 2
    c_cw, c_ccw = cut((y_next,), [[(0, y_rows - c_rows, c_rows)], [(0, 2 * y_rows - c_rows, c_rows)]])
    cw, ccw = send(to_cw, cw_pairs), send(to_ccw, ccw_pairs)
    y_next = send(y_message, other_y)
    c_cw, c_ccw = send(c_cw, cw_pairs), send(c_ccw, ccw_pairs)
    work(items)
    cw, ccw = after(cw), after(ccw)
    work([(cw, ((1, hops, "half"),)), (ccw, ((-1, hops, "half"),))])
    items = [
        (c_cw, ((1, hops - 1, "c"),)),
        (c_ccw, ((-1, hops - 1, "c"),)),
        (y_next, ((1, hops - 1, "y_last"), (-1, hops - 1, "y_last"))),
    ]
    pieces, meta = zip(*items)
    packed = stats_of(
        pieces, meta, head, other_head, *sizes, earlier=tuple(metas), stats=stats, tail=True
    )
    received = lax.all_to_all(packed, AXES, 0, 0, tiled=True)
    return finish(received, lengths)


def solution(mesh):
    n_req, n_tp = mesh.shape["req"], mesh.shape["tp"]
    in_specs = (P("req", None), P(), P(None, ("req", "tp")), P("req"), P("req"))
    out_specs = (P("req"), P("req"), P("req"), P("req"))
    return jax.shard_map(
        functools.partial(per_device, n_req, n_tp),
        mesh=mesh,
        in_specs=in_specs,
        out_specs=out_specs,
        check_vma=False,
    )
```

```python
import functools
import math

import jax
import jax.numpy as jnp
from jax import lax
from jax.experimental import pallas as pl
from jax.experimental.pallas import tpu as pltpu
from jax.sharding import PartitionSpec as P

AXES = ("req", "tp")
LANES = 128
STATS = 4
DIGIT_BITS = 7
CHUNKS = 1
VMEM_BYTES = 10 * 1024 * 1024


def ring_place(req, n_req):
    half = n_req // 2
    return jnp.where(req % 2 == 0, req // 2, n_req - 1 - req // 2) if half else req


def ring_req(place, n_req):
    half = n_req // 2
    return jnp.where(place < half, 2 * place, 2 * (n_req - 1 - place) + 1)


def ring_req_py(place, n_req):
    place %= n_req
    return 2 * place if place < n_req // 2 else 2 * (n_req - 1 - place) + 1


def ring_pairs(n_req, n_tp, turn):
    pairs = []
    for place in range(n_req):
        here, there = ring_req_py(place, n_req), ring_req_py(place + turn, n_req)
        pairs += [(here * n_tp + t, there * n_tp + t) for t in range(n_tp)]
    return pairs


def tp_pairs(n_req, n_tp, bit):
    return [(r * n_tp + t, r * n_tp + (t ^ bit)) for r in range(n_req) for t in range(n_tp)]


def segments(rows):
    e = rows // 8
    return (0, 2 * e, 3 * e, 4 * e, 5 * e, 6 * e), (2 * e, e, e, e, e, 2 * e)


PARTS = {
    "all": (0, 1, 2, 3, 4, 5),
    "most": (0, 1, 2, 3),
    "half": (0, 1, 2),
    "y": (5, 4),
    "y_last": (5,),
    "c": (4,),
}


def shard_index(turn, hops, n_req):
    return hops if turn >= 0 or 2 * hops == n_req else n_req // 2 + hops


def part_rows(part, rows):
    return sum(segments(rows)[1][j] for j in PARTS[part])


def digits(target):
    lane = lax.broadcasted_iota(jnp.int32, (1, LANES), 1)
    shift = jnp.where(lane == 0, 2 * DIGIT_BITS, jnp.where(lane == 1, DIGIT_BITS, 0))
    digit = (target >> shift) & ((1 << DIGIT_BITS) - 1)
    return jnp.where(lane < 3, digit, 0).astype(jnp.float32).astype(jnp.bfloat16)


def undigits(ext):
    lane = lax.broadcasted_iota(jnp.int32, (1, LANES), 1)
    base = float(1 << DIGIT_BITS)
    weight = jnp.where(
        lane == 0, base * base, jnp.where(lane == 1, base, jnp.where(lane == 2, 1.0, 0.0))
    )
    return jnp.sum(ext.astype(jnp.float32) * weight, axis=1, keepdims=True)


def norm_kernel(x_hbm, gain_hbm, tid_hbm, xn_ref, cw_ref, ccw_ref, x_ref, gain_ref, tid_ref, sems):
    rows, d = x_ref.shape
    tp = lax.axis_index("tp")
    core, plane = tp % 2, tp // 2
    size = rows // CHUNKS
    get_gain = pltpu.make_async_copy(gain_hbm, gain_ref, sems.at[CHUNKS])
    get_tid = pltpu.make_async_copy(tid_hbm, tid_ref, sems.at[CHUNKS + 1])
    get_gain.start()
    get_tid.start()
    chunks = []
    for k in range(CHUNKS):
        there = pl.ds(pl.multiple_of(core * rows + k * size, size), size)
        here = pl.ds(k * size, size)
        chunks.append(pltpu.make_async_copy(x_hbm.at[there, :], x_ref.at[here, :], sems.at[k]))
        chunks[k].start()
    get_tid.wait()
    target = jnp.where(core == 0, tid_ref[0:1, :], tid_ref[1:2, :])
    xn_ref[:, d:] = digits(jnp.broadcast_to(target, (8, rows)).T[:, :1])
    get_gain.wait()
    for k in range(CHUNKS):
        chunks[k].wait()
        here = pl.ds(k * size, size)
        feats = x_ref[here, :].astype(jnp.float32)
        scale = lax.rsqrt(jnp.mean(feats * feats, axis=-1, keepdims=True) + 1e-06)
        xn_ref[here, :d] = (feats * scale * gain_ref[...]).astype(jnp.bfloat16)
    starts, sizes = segments(rows)
    for ref, flip in ((cw_ref, 0), (ccw_ref, 1)):
        down = plane != flip
        at = 0
        for j in PARTS["most"]:
            start = pl.multiple_of(jnp.where(down, starts[5 - j], starts[j]), 16)
            ref[pl.ds(at, sizes[j]), :] = xn_ref[pl.ds(start, sizes[j]), :]
            at += sizes[j]


def norm_rows(hidden, norm_gain, target_ids, rows):
    d = hidden.shape[1]
    wide = d + LANES
    message = (part_rows("most", rows), wide)
    shapes = [(rows, wide), message, message]
    hbm_operands = (hidden, norm_gain.reshape(1, d), target_ids.reshape(2, rows))
    return pl.pallas_call(
        norm_kernel,
        out_shape=[jax.ShapeDtypeStruct(s, jnp.bfloat16) for s in shapes],
        in_specs=[pl.BlockSpec(memory_space=pl.ANY)] * 3,
        scratch_shapes=[
            pltpu.VMEM((rows, d), jnp.bfloat16),
            pltpu.VMEM((1, d), jnp.float32),
            pltpu.VMEM((2, rows), jnp.int32),
            pltpu.SemaphoreType.DMA((CHUNKS + 2,)),
        ],
        compiler_params=pltpu.CompilerParams(vmem_limit_bytes=VMEM_BYTES),
        name="norm",
    )(*(pltpu.with_memory_space_constraint(v, pltpu.HBM) for v in hbm_operands))


def cut_kernel(plan, n_in, *refs):
    for out_ref, pieces in zip(refs[n_in:], plan):
        to = 0
        for k, at, count in pieces:
            out_ref[pl.ds(to, count), :] = refs[k][pl.ds(at, count), :]
            to += count


def cut(arrays, plan):
    wide = arrays[0].shape[1]
    return pl.pallas_call(
        functools.partial(cut_kernel, plan, len(arrays)),
        out_shape=[
            jax.ShapeDtypeStruct((sum(count for _, _, count in pieces), wide), arrays[0].dtype)
            for pieces in plan
        ],
        compiler_params=pltpu.CompilerParams(vmem_limit_bytes=VMEM_BYTES),
        name="cut",
    )(*arrays)


def stats_kernel(metas, n_req, n_tp, rows, earlier, tail, *refs):
    n = len(metas)
    piece_refs, (w0_ref, w1_ref), refs = refs[:n], refs[n : n + 2], refs[n + 2 :]
    if tail:
        stat_refs, refs = refs[: len(earlier)], refs[len(earlier) :]
        packed_ref, x_s, l_s, t_s, out_ref = refs
    else:
        out_ref, x_s, l_s, t_s = refs
    req, tp = lax.axis_index("req"), lax.axis_index("tp")
    d, vdev = w0_ref.shape
    total = x_s.shape[0]

    lane = lax.broadcasted_iota(jnp.int32, (1, LANES), 1)
    at = 0
    for parts, ref in zip(metas, piece_refs):
        here = pl.ds(at, ref.shape[0])
        x_s[here, :] = ref[:, :d]
        t_s[here, :] = undigits(ref[:, d:])
        at += ref.shape[0]

    x = x_s[...]
    l_s[:, :vdev] = jnp.dot(x, w0_ref[...], preferred_element_type=jnp.float32)
    l_s[:, vdev:] = jnp.dot(x, w1_ref[...], preferred_element_type=jnp.float32)

    column = lax.broadcasted_iota(jnp.int32, (1, vdev), 1)
    ids0 = (column + (req * n_tp + tp) * vdev).astype(jnp.float32)
    ids1 = (column + (req * n_tp + (tp ^ 1)) * vdev).astype(jnp.float32)
    step = math.gcd(total, 32)

    def body(i, _):
        here = pl.ds(pl.multiple_of(i * step, step), step)
        logits = l_s[here, :]
        target = t_s[here, :]
        top = jnp.max(logits, axis=1, keepdims=True)
        shifted = jnp.exp(logits - top)
        weight_sum = jnp.sum(shifted, axis=1, keepdims=True)
        weighted = jnp.sum(shifted * logits, axis=1, keepdims=True)
        hit0 = jnp.where(ids0 == target, logits[:, :vdev], 0.0)
        hit1 = jnp.where(ids1 == target, logits[:, vdev:], 0.0)
        picked = jnp.sum(hit0 + hit1, axis=1, keepdims=True)
        values = jnp.where(lane == 3, picked, 0.0)
        values = jnp.where(lane == 2, weighted, values)
        values = jnp.where(lane == 1, weight_sum, values)
        out_ref[here, :] = jnp.where(lane == 0, top, values)
        return 0

    lax.fori_loop(0, total // step, body, 0, unroll=total // step)
    at = 0
    for turn, hops, part in (p for parts in metas for p in parts):
        here = pl.ds(at, part_rows(part, rows))
        at += part_rows(part, rows)
        if hops:
            first = STATS * shard_index(turn, hops, n_req)
            out_ref[here, :] = pltpu.roll(out_ref[here, :], first, 1)
    if tail:
        pack_stats(earlier + (metas,), (*stat_refs, out_ref), packed_ref, n_req, n_tp, rows)


def pack_stats(metas, stat_refs, packed_ref, n_req, n_tp, rows):
    plane = lax.axis_index("tp") // 2
    place = ring_place(lax.axis_index("req"), n_req)
    _, sizes = segments(rows)
    own, found = None, [[] for _ in sizes]
    for pieces, ref in zip(metas, stat_refs):
        at = 0
        for turn, hops, part in (p for parts in pieces for p in parts):
            for j in PARTS[part]:
                here = ref[pl.ds(at, sizes[j]), :]
                at += sizes[j]
                if hops:
                    found[j if turn > 0 else 5 - j].append(here)
                else:
                    own = ref[...]
    found = [functools.reduce(jnp.add, values) for values in found]
    total = own + jnp.where(
        plane == 0, jnp.concatenate(found, axis=0), jnp.concatenate(found[::-1], axis=0)
    )
    lanes = total.T
    turns = [(0, 0)] + [(1, h) for h in range(1, n_req // 2 + 1)]
    for turn, hops in turns + [(-1, h) for h in range(1, n_req // 2)]:
        source = ring_req((place - turn * hops + n_req) % n_req, n_req)
        k = STATS * shard_index(turn, hops, n_req)
        for t in range(n_tp):
            packed_ref[source * n_tp + t] = lanes[k : k + STATS, :]


def stats_of(pieces, metas, w0, w1, n_req, n_tp, rows, earlier=(), stats=(), tail=False):
    d, vdev = w0.shape
    total = sum(p.shape[0] for p in pieces)
    row_stats = (total, LANES)
    return pl.pallas_call(
        functools.partial(stats_kernel, metas, n_req, n_tp, rows, earlier, tail),
        out_shape=jax.ShapeDtypeStruct(
            (n_req * n_tp, STATS, rows) if tail else row_stats, jnp.float32
        ),
        scratch_shapes=[
            pltpu.VMEM((total, d), jnp.bfloat16),
            pltpu.VMEM((total, 2 * vdev), jnp.float32),
            pltpu.VMEM((total, 1), jnp.float32),
        ]
        + [pltpu.VMEM(row_stats, jnp.float32)] * tail,
        compiler_params=pltpu.CompilerParams(vmem_limit_bytes=VMEM_BYTES),
        cost_estimate=pl.CostEstimate(
            flops=4 * total * d * vdev, bytes_accessed=4 * d * vdev, transcendentals=2 * total * vdev
        ),
        name="stats_last" if tail else "stats",
    )(*pieces, w0, w1, *stats)


def final_kernel(n_parts, r_ref, len_ref, lp_ref, ent_ref, mean_ref, top_ref):
    rows = r_ref.shape[2]
    length = len_ref[0]
    total = jnp.float32(0.0)
    best = jnp.float32(-1e30)
    for half in range(2):
        mine = [r_ref[2 * k + half] for k in range(n_parts // 2)]
        top = functools.reduce(jnp.maximum, [m[0:1] for m in mine])
        scaled = functools.reduce(jnp.add, [m * jnp.exp(m[0:1] - top) for m in mine])
        picked = functools.reduce(jnp.add, [m[3:4] for m in mine])
        weight_sum, weighted = scaled[1:2], scaled[2:3]
        log_norm = top + jnp.log(weight_sum)
        slot = lax.broadcasted_iota(jnp.int32, (1, rows), 1) + half * rows
        live = slot < length
        logprob = jnp.where(live, picked - log_norm, 0.0)
        lp_ref[half : half + 1, :] = logprob
        ent_ref[half : half + 1, :] = jnp.where(live, log_norm - weighted / weight_sum, 0.0)
        total += jnp.sum(logprob)
        best = jnp.maximum(best, jnp.max(jnp.where(live, top, -1e30)))
    mean_ref[...] = jnp.full((1, 1), total, jnp.float32) / length.astype(jnp.float32)
    top_ref[...] = jnp.full((1, 1), best, jnp.float32)


def finish(received, lengths):
    n_parts, _, rows = received.shape
    outs = pl.pallas_call(
        functools.partial(final_kernel, n_parts),
        out_shape=[jax.ShapeDtypeStruct((2, rows), jnp.float32)] * 2
        + [jax.ShapeDtypeStruct((1, 1), jnp.float32)] * 2,
        in_specs=[
            pl.BlockSpec(memory_space=pltpu.VMEM),
            pl.BlockSpec(memory_space=pltpu.SMEM),
        ],
        compiler_params=pltpu.CompilerParams(vmem_limit_bytes=VMEM_BYTES),
        name="finish",
    )(received, lengths)
    return tuple(o.reshape(-1) for o in outs)


def per_device(n_req, n_tp, hidden_states, norm_gain, head, target_ids, lengths):
    rows = hidden_states.shape[0] // 2
    cw_pairs, ccw_pairs = ring_pairs(n_req, n_tp, 1), ring_pairs(n_req, n_tp, -1)
    other_core, other_y = tp_pairs(n_req, n_tp, 1), tp_pairs(n_req, n_tp, 2)
    sizes = (n_req, n_tp, rows)
    y_rows, c_rows, half = (part_rows(part, rows) for part in ("y", "c", "half"))
    y_last_rows = part_rows("y_last", rows)
    metas, stats = [], []

    def send(value, pairs):
        return lax.ppermute(value, AXES, pairs)

    def work(items):
        pieces, meta = zip(*items)
        stats.append(stats_of(pieces, meta, head, other_head, *sizes))
        metas.append(meta)

    def after(value):
        value, stats[-1] = lax.optimization_barrier((value, stats[-1]))
        return value

    xn, to_cw, to_ccw = norm_rows(hidden_states, norm_gain, target_ids, rows)
    swapped, xn = lax.optimization_barrier((head, xn))
    other_head = send(swapped, other_core)
    items = [(xn, ((0, 0, "all"),))]
    for hops in range(1, n_req // 2):
        next_to_last = 2 * hops + 2 == n_req
        cw, ccw = send(to_cw, cw_pairs), send(to_ccw, ccw_pairs)
        if hops > 1:
            y_next = send(y_message, other_y)
        work(items)
        cw, ccw = after(cw), after(ccw)
        items = [(cw, ((1, hops, "most"),)), (ccw, ((-1, hops, "most"),))]
        if hops > 1:
            items.append((y_next, ((1, hops - 1, "y"), (-1, hops - 1, "y"))))
        if next_to_last:
            (to_cw,), (to_ccw,) = cut((cw,), [[(0, 0, half)]]), cut((ccw,), [[(0, 0, half)]])
        else:
            to_cw, to_ccw = cw, ccw
        count = y_last_rows if next_to_last else y_rows
        (y_message,) = cut((cw, ccw), [[(0, 0, count), (1, 0, count)]])
    hops = n_req // 2
    c_cw, c_ccw = cut((y_next,), [[(0, y_rows - c_rows, c_rows)], [(0, 2 * y_rows - c_rows, c_rows)]])
    cw, ccw = send(to_cw, cw_pairs), send(to_ccw, ccw_pairs)
    y_next = send(y_message, other_y)
    c_cw, c_ccw = send(c_cw, cw_pairs), send(c_ccw, ccw_pairs)
    work(items)
    cw, ccw = after(cw), after(ccw)
    work([(cw, ((1, hops, "half"),)), (ccw, ((-1, hops, "half"),))])
    items = [
        (c_cw, ((1, hops - 1, "c"),)),
        (c_ccw, ((-1, hops - 1, "c"),)),
        (y_next, ((1, hops - 1, "y_last"), (-1, hops - 1, "y_last"))),
    ]
    pieces, meta = zip(*items)
    packed = stats_of(
        pieces, meta, head, other_head, *sizes, earlier=tuple(metas), stats=stats, tail=True
    )
    received = lax.all_to_all(packed, AXES, 0, 0, tiled=True)
    return finish(received, lengths)


def solution(mesh):
    n_req, n_tp = mesh.shape["req"], mesh.shape["tp"]
    in_specs = (P("req", None), P(), P(None, ("req", "tp")), P("req"), P("req"))
    out_specs = (P("req"), P("req"), P("req"), P("req"))
    return jax.shard_map(
        functools.partial(per_device, n_req, n_tp),
        mesh=mesh,
        in_specs=in_specs,
        out_specs=out_specs,
        check_vma=False,
    )
```

```python
import functools
import math

import jax
import jax.numpy as jnp
from jax import lax
from jax.experimental import pallas as pl
from jax.experimental.pallas import tpu as pltpu
from jax.sharding import PartitionSpec as P

AXES = ("req", "tp")
LANES = 128
STATS = 4
DIGIT_BITS = 7
NOTHING = -1e30
EARLY_ROWS = 32
VMEM_BYTES = 10 * 1024 * 1024


def ring_place(req, n_req):
    half = n_req // 2
    return jnp.where(req % 2 == 0, req // 2, n_req - 1 - req // 2) if half else req


def ring_req(place, n_req):
    half = n_req // 2
    return jnp.where(place < half, 2 * place, 2 * (n_req - 1 - place) + 1)


def ring_req_py(place, n_req):
    place %= n_req
    return 2 * place if place < n_req // 2 else 2 * (n_req - 1 - place) + 1


def ring_pairs(n_req, n_tp, turn):
    pairs = []
    for place in range(n_req):
        here, there = ring_req_py(place, n_req), ring_req_py(place + turn, n_req)
        pairs += [(here * n_tp + t, there * n_tp + t) for t in range(n_tp)]
    return pairs


def tp_pairs(n_req, n_tp, bit):
    return [(r * n_tp + t, r * n_tp + (t ^ bit)) for r in range(n_req) for t in range(n_tp)]


def segments(rows):
    e = rows // 8
    return (0, 2 * e, 3 * e, 4 * e, 5 * e, 6 * e), (2 * e, e, e, e, e, 2 * e)


PARTS = {
    "all": (0, 1, 2, 3, 4, 5),
    "most": (0, 1, 2, 3),
    "half": (0, 1, 2),
    "y": (5, 4),
    "y_last": (5,),
    "c": (4,),
}


def shard_index(turn, hops, n_req):
    return hops if turn >= 0 or 2 * hops == n_req else n_req // 2 + hops


def part_rows(part, rows):
    return sum(segments(rows)[1][j] for j in PARTS[part])


def digits(target):
    lane = lax.broadcasted_iota(jnp.int32, (1, LANES), 1)
    shift = jnp.where(lane == 0, 2 * DIGIT_BITS, jnp.where(lane == 1, DIGIT_BITS, 0))
    digit = (target >> shift) & ((1 << DIGIT_BITS) - 1)
    return jnp.where(lane < 3, digit, 0).astype(jnp.float32).astype(jnp.bfloat16)


def undigits(ext):
    lane = lax.broadcasted_iota(jnp.int32, (1, LANES), 1)
    base = float(1 << DIGIT_BITS)
    weight = jnp.where(
        lane == 0, base * base, jnp.where(lane == 1, base, jnp.where(lane == 2, 1.0, 0.0))
    )
    return jnp.sum(ext.astype(jnp.float32) * weight, axis=1, keepdims=True)


def row_stats(logits, target, ids):
    lane = lax.broadcasted_iota(jnp.int32, (1, LANES), 1)
    top = jnp.max(logits, axis=1, keepdims=True)
    shifted = jnp.exp(logits - top)
    weight_sum = jnp.sum(shifted, axis=1, keepdims=True)
    weighted = jnp.sum(shifted * logits, axis=1, keepdims=True)
    width = logits.shape[1] // len(ids)
    hits = [
        jnp.where(part == target, logits[:, k * width : (k + 1) * width], 0.0)
        for k, part in enumerate(ids)
    ]
    picked = jnp.sum(functools.reduce(jnp.add, hits), axis=1, keepdims=True)
    values = jnp.where(lane == 3, picked, 0.0)
    values = jnp.where(lane == 2, weighted, values)
    values = jnp.where(lane == 1, weight_sum, values)
    return jnp.where(lane == 0, top, values)


def vocab_ids(vdev, owner):
    column = lax.broadcasted_iota(jnp.int32, (1, vdev), 1)
    return (column + owner * vdev).astype(jnp.float32)


def norm_kernel(
    n_tp, x_hbm, gain_hbm, tid_hbm, head_hbm, xn_ref, cw_ref, ccw_ref, early_ref,
    x_ref, gain_ref, tid_ref, head_ref, sems,
):
    rows, d = x_ref.shape
    vdev = head_ref.shape[1]
    req, tp = lax.axis_index("req"), lax.axis_index("tp")
    core, plane = tp % 2, tp // 2
    mine = pl.ds(pl.multiple_of(core * rows, rows), rows)
    get_x = pltpu.make_async_copy(x_hbm.at[mine, :], x_ref, sems.at[0])
    get_gain = pltpu.make_async_copy(gain_hbm, gain_ref, sems.at[1])
    get_tid = pltpu.make_async_copy(tid_hbm, tid_ref, sems.at[2])
    get_x.start()
    get_gain.start()
    get_tid.start()
    get_tid.wait()
    target = jnp.where(core == 0, tid_ref[0:1, :], tid_ref[1:2, :])
    target = jnp.broadcast_to(target, (8, rows)).T[:, :1]
    xn_ref[:, d:] = digits(target)
    get_gain.wait()
    get_x.wait()
    feats = x_ref[...].astype(jnp.float32)
    scale = lax.rsqrt(jnp.mean(feats * feats, axis=-1, keepdims=True) + 1e-06)
    xn_ref[:, :d] = (feats * scale * gain_ref[...]).astype(jnp.bfloat16)

    @pl.when(core == 0)
    def _():
        lane = lax.broadcasted_iota(jnp.int32, (rows, LANES), 1)
        early_ref[...] = jnp.where(lane == 0, NOTHING, 0.0)

    @pl.when(core == 1)
    def _():
        get_head = pltpu.make_async_copy(head_hbm, head_ref, sems.at[3])
        get_head.start()
        get_head.wait()
        ids = [vocab_ids(vdev, req * n_tp + tp)]
        for k in range(0, rows, EARLY_ROWS):
            logits = jnp.dot(
                xn_ref[k : k + EARLY_ROWS, :d], head_ref[...], preferred_element_type=jnp.float32
            )
            wanted = undigits(xn_ref[k : k + EARLY_ROWS, d:])
            early_ref[k : k + EARLY_ROWS, :] = row_stats(logits, wanted, ids)

    starts, sizes = segments(rows)
    for ref, flip in ((cw_ref, 0), (ccw_ref, 1)):
        down = plane != flip
        at = 0
        for j in PARTS["most"]:
            start = pl.multiple_of(jnp.where(down, starts[5 - j], starts[j]), 16)
            ref[pl.ds(at, sizes[j]), :] = xn_ref[pl.ds(start, sizes[j]), :]
            at += sizes[j]


def norm_rows(hidden, norm_gain, target_ids, head, n_tp, rows):
    d = hidden.shape[1]
    wide = d + LANES
    message = (part_rows("most", rows), wide)
    hbm_operands = (hidden, norm_gain.reshape(1, d), target_ids.reshape(2, rows), head)
    return pl.pallas_call(
        functools.partial(norm_kernel, n_tp),
        out_shape=[jax.ShapeDtypeStruct(s, jnp.bfloat16) for s in [(rows, wide), message, message]]
        + [jax.ShapeDtypeStruct((rows, LANES), jnp.float32)],
        in_specs=[pl.BlockSpec(memory_space=pl.ANY)] * 4,
        scratch_shapes=[
            pltpu.VMEM((rows, d), jnp.bfloat16),
            pltpu.VMEM((1, d), jnp.float32),
            pltpu.VMEM((2, rows), jnp.int32),
            pltpu.VMEM(head.shape, head.dtype),
            pltpu.SemaphoreType.DMA((4,)),
        ],
        compiler_params=pltpu.CompilerParams(vmem_limit_bytes=VMEM_BYTES),
        name="norm",
    )(*(pltpu.with_memory_space_constraint(v, pltpu.HBM) for v in hbm_operands))


def cut_kernel(plan, n_in, *refs):
    for out_ref, pieces in zip(refs[n_in:], plan):
        to = 0
        for k, at, count in pieces:
            out_ref[pl.ds(to, count), :] = refs[k][pl.ds(at, count), :]
            to += count


def cut(arrays, plan):
    wide = arrays[0].shape[1]
    return pl.pallas_call(
        functools.partial(cut_kernel, plan, len(arrays)),
        out_shape=[
            jax.ShapeDtypeStruct((sum(count for _, _, count in pieces), wide), arrays[0].dtype)
            for pieces in plan
        ],
        compiler_params=pltpu.CompilerParams(vmem_limit_bytes=VMEM_BYTES),
        name="cut",
    )(*arrays)


def stats_kernel(metas, n_req, n_tp, rows, earlier, tail, first, *refs):
    n = len(metas)
    piece_refs, (w0_ref, w1_ref), refs = refs[:n], refs[n : n + 2], refs[n + 2 :]
    if first:
        early_ref, refs = refs[0], refs[1:]
    if tail:
        stat_refs, refs = refs[: len(earlier)], refs[len(earlier) :]
        packed_ref, x_s, l_s, t_s, out_ref = refs
    else:
        out_ref, x_s, l_s, t_s = refs
    req, tp = lax.axis_index("req"), lax.axis_index("tp")
    d, vdev = w0_ref.shape
    total = x_s.shape[0]

    lane = lax.broadcasted_iota(jnp.int32, (1, LANES), 1)
    at = 0
    for parts, ref in zip(metas, piece_refs):
        here = pl.ds(at, ref.shape[0])
        x_s[here, :] = ref[:, :d]
        t_s[here, :] = undigits(ref[:, d:])
        at += ref.shape[0]

    own = tp % 2 == 0 if first else True
    ids = [vocab_ids(vdev, req * n_tp + tp), vocab_ids(vdev, req * n_tp + (tp ^ 1))]
    x = x_s[...]
    l_s[:, vdev:] = jnp.dot(x, w1_ref[...], preferred_element_type=jnp.float32)
    if first:

        @pl.when(own)
        def _():
            l_s[:, :vdev] = jnp.dot(x_s[...], w0_ref[...], preferred_element_type=jnp.float32)

        @pl.when(jnp.logical_not(own))
        def _():
            l_s[:, :vdev] = jnp.full((total, vdev), NOTHING, jnp.float32)

        ids[0] = jnp.where(own, ids[0], -1.0)
    else:
        l_s[:, :vdev] = jnp.dot(x, w0_ref[...], preferred_element_type=jnp.float32)
    step = math.gcd(total, 32)

    def body(i, _):
        here = pl.ds(pl.multiple_of(i * step, step), step)
        out_ref[here, :] = row_stats(l_s[here, :], t_s[here, :], ids)
        return 0

    lax.fori_loop(0, total // step, body, 0, unroll=total // step)
    if first:
        out_ref[...] = merged(out_ref[...], early_ref[...])
    at = 0
    for turn, hops, part in (p for parts in metas for p in parts):
        here = pl.ds(at, part_rows(part, rows))
        at += part_rows(part, rows)
        if hops:
            first = STATS * shard_index(turn, hops, n_req)
            out_ref[here, :] = pltpu.roll(out_ref[here, :], first, 1)
    if tail:
        pack_stats(earlier + (metas,), (*stat_refs, out_ref), packed_ref, n_req, n_tp, rows)


def merged(one, two):
    lane = lax.broadcasted_iota(jnp.int32, (1, LANES), 1)
    top = jnp.maximum(one[:, :1], two[:, :1])
    scaled = one * jnp.exp(one[:, :1] - top) + two * jnp.exp(two[:, :1] - top)
    return jnp.where(lane == 0, top, jnp.where(lane == 3, one + two, scaled))


def pack_stats(metas, stat_refs, packed_ref, n_req, n_tp, rows):
    plane = lax.axis_index("tp") // 2
    place = ring_place(lax.axis_index("req"), n_req)
    _, sizes = segments(rows)
    own, found = None, [[] for _ in sizes]
    for pieces, ref in zip(metas, stat_refs):
        at = 0
        for turn, hops, part in (p for parts in pieces for p in parts):
            for j in PARTS[part]:
                here = ref[pl.ds(at, sizes[j]), :]
                at += sizes[j]
                if hops:
                    found[j if turn > 0 else 5 - j].append(here)
                else:
                    own = ref[...]
    found = [functools.reduce(jnp.add, values) for values in found]
    total = own + jnp.where(
        plane == 0, jnp.concatenate(found, axis=0), jnp.concatenate(found[::-1], axis=0)
    )
    lanes = total.T
    turns = [(0, 0)] + [(1, h) for h in range(1, n_req // 2 + 1)]
    for turn, hops in turns + [(-1, h) for h in range(1, n_req // 2)]:
        source = ring_req((place - turn * hops + n_req) % n_req, n_req)
        k = STATS * shard_index(turn, hops, n_req)
        for t in range(n_tp):
            packed_ref[source * n_tp + t] = lanes[k : k + STATS, :]


def stats_of(
    pieces, metas, w0, w1, n_req, n_tp, rows, early=(), earlier=(), stats=(), tail=False
):
    d, vdev = w0.shape
    total = sum(p.shape[0] for p in pieces)
    row_stats = (total, LANES)
    return pl.pallas_call(
        functools.partial(
            stats_kernel, metas, n_req, n_tp, rows, earlier, tail, len(early) > 0
        ),
        out_shape=jax.ShapeDtypeStruct(
            (n_req * n_tp, STATS, rows) if tail else row_stats, jnp.float32
        ),
        scratch_shapes=[
            pltpu.VMEM((total, d), jnp.bfloat16),
            pltpu.VMEM((total, 2 * vdev), jnp.float32),
            pltpu.VMEM((total, 1), jnp.float32),
        ]
        + [pltpu.VMEM(row_stats, jnp.float32)] * tail,
        compiler_params=pltpu.CompilerParams(vmem_limit_bytes=VMEM_BYTES),
        cost_estimate=pl.CostEstimate(
            flops=4 * total * d * vdev, bytes_accessed=4 * d * vdev, transcendentals=2 * total * vdev
        ),
        name="stats_last" if tail else "stats",
    )(*pieces, w0, w1, *early, *stats)


def final_kernel(n_parts, r_ref, len_ref, lp_ref, ent_ref, mean_ref, top_ref):
    rows = r_ref.shape[2]
    length = len_ref[0]
    total = jnp.float32(0.0)
    best = jnp.float32(-1e30)
    for half in range(2):
        mine = [r_ref[2 * k + half] for k in range(n_parts // 2)]
        top = functools.reduce(jnp.maximum, [m[0:1] for m in mine])
        scaled = functools.reduce(jnp.add, [m * jnp.exp(m[0:1] - top) for m in mine])
        picked = functools.reduce(jnp.add, [m[3:4] for m in mine])
        weight_sum, weighted = scaled[1:2], scaled[2:3]
        log_norm = top + jnp.log(weight_sum)
        slot = lax.broadcasted_iota(jnp.int32, (1, rows), 1) + half * rows
        live = slot < length
        logprob = jnp.where(live, picked - log_norm, 0.0)
        lp_ref[half : half + 1, :] = logprob
        ent_ref[half : half + 1, :] = jnp.where(live, log_norm - weighted / weight_sum, 0.0)
        total += jnp.sum(logprob)
        best = jnp.maximum(best, jnp.max(jnp.where(live, top, -1e30)))
    mean_ref[...] = jnp.full((1, 1), total, jnp.float32) / length.astype(jnp.float32)
    top_ref[...] = jnp.full((1, 1), best, jnp.float32)


def finish(received, lengths):
    n_parts, _, rows = received.shape
    outs = pl.pallas_call(
        functools.partial(final_kernel, n_parts),
        out_shape=[jax.ShapeDtypeStruct((2, rows), jnp.float32)] * 2
        + [jax.ShapeDtypeStruct((1, 1), jnp.float32)] * 2,
        in_specs=[
            pl.BlockSpec(memory_space=pltpu.VMEM),
            pl.BlockSpec(memory_space=pltpu.SMEM),
        ],
        compiler_params=pltpu.CompilerParams(vmem_limit_bytes=VMEM_BYTES),
        name="finish",
    )(received, lengths)
    return tuple(o.reshape(-1) for o in outs)


def per_device(n_req, n_tp, hidden_states, norm_gain, head, target_ids, lengths):
    rows = hidden_states.shape[0] // 2
    cw_pairs, ccw_pairs = ring_pairs(n_req, n_tp, 1), ring_pairs(n_req, n_tp, -1)
    other_core, other_y = tp_pairs(n_req, n_tp, 1), tp_pairs(n_req, n_tp, 2)
    sizes = (n_req, n_tp, rows)
    y_rows, c_rows, half = (part_rows(part, rows) for part in ("y", "c", "half"))
    y_last_rows = part_rows("y_last", rows)
    metas, stats = [], []

    def send(value, pairs):
        return lax.ppermute(value, AXES, pairs)

    def work(items, early=()):
        pieces, meta = zip(*items)
        stats.append(stats_of(pieces, meta, head, other_head, *sizes, early=early))
        metas.append(meta)

    def after(value):
        value, stats[-1] = lax.optimization_barrier((value, stats[-1]))
        return value

    other_head = send(head, other_core)
    xn, to_cw, to_ccw, early = norm_rows(
        hidden_states, norm_gain, target_ids, head, n_tp, rows
    )
    items = [(xn, ((0, 0, "all"),))]
    for hops in range(1, n_req // 2):
        next_to_last = 2 * hops + 2 == n_req
        cw, ccw = send(to_cw, cw_pairs), send(to_ccw, ccw_pairs)
        if hops > 1:
            y_next = send(y_message, other_y)
        work(items, () if stats else (early,))
        cw, ccw = after(cw), after(ccw)
        items = [(cw, ((1, hops, "most"),)), (ccw, ((-1, hops, "most"),))]
        if hops > 1:
            items.append((y_next, ((1, hops - 1, "y"), (-1, hops - 1, "y"))))
        if next_to_last:
            (to_cw,), (to_ccw,) = cut((cw,), [[(0, 0, half)]]), cut((ccw,), [[(0, 0, half)]])
        else:
            to_cw, to_ccw = cw, ccw
        count = y_last_rows if next_to_last else y_rows
        (y_message,) = cut((cw, ccw), [[(0, 0, count), (1, 0, count)]])
    hops = n_req // 2
    c_cw, c_ccw = cut((y_next,), [[(0, y_rows - c_rows, c_rows)], [(0, 2 * y_rows - c_rows, c_rows)]])
    cw, ccw = send(to_cw, cw_pairs), send(to_ccw, ccw_pairs)
    y_next = send(y_message, other_y)
    c_cw, c_ccw = send(c_cw, cw_pairs), send(c_ccw, ccw_pairs)
    work(items)
    cw, ccw = after(cw), after(ccw)
    work([(cw, ((1, hops, "half"),)), (ccw, ((-1, hops, "half"),))])
    items = [
        (c_cw, ((1, hops - 1, "c"),)),
        (c_ccw, ((-1, hops - 1, "c"),)),
        (y_next, ((1, hops - 1, "y_last"), (-1, hops - 1, "y_last"))),
    ]
    pieces, meta = zip(*items)
    packed = stats_of(
        pieces, meta, head, other_head, *sizes, earlier=tuple(metas), stats=stats, tail=True
    )
    received = lax.all_to_all(packed, AXES, 0, 0, tiled=True)
    return finish(received, lengths)


def solution(mesh):
    n_req, n_tp = mesh.shape["req"], mesh.shape["tp"]
    in_specs = (P("req", None), P(), P(None, ("req", "tp")), P("req"), P("req"))
    out_specs = (P("req"), P("req"), P("req"), P("req"))
    return jax.shard_map(
        functools.partial(per_device, n_req, n_tp),
        mesh=mesh,
        in_specs=in_specs,
        out_specs=out_specs,
        check_vma=False,
    )
```

```python
import functools
import math

import jax
import jax.numpy as jnp
from jax import lax
from jax.experimental import pallas as pl
from jax.experimental.pallas import tpu as pltpu
from jax.sharding import PartitionSpec as P

AXES = ("req", "tp")
LANES = 128
STATS = 4
DIGIT_BITS = 7
NOTHING = -1e30
EARLY_TILES = (32, 32, 16, 16, 16, 16)
VMEM_BYTES = 10 * 1024 * 1024


def ring_place(req, n_req):
    half = n_req // 2
    return jnp.where(req % 2 == 0, req // 2, n_req - 1 - req // 2) if half else req


def ring_req(place, n_req):
    half = n_req // 2
    return jnp.where(place < half, 2 * place, 2 * (n_req - 1 - place) + 1)


def ring_req_py(place, n_req):
    place %= n_req
    return 2 * place if place < n_req // 2 else 2 * (n_req - 1 - place) + 1


def ring_pairs(n_req, n_tp, turn):
    pairs = []
    for place in range(n_req):
        here, there = ring_req_py(place, n_req), ring_req_py(place + turn, n_req)
        pairs += [(here * n_tp + t, there * n_tp + t) for t in range(n_tp)]
    return pairs


def tp_pairs(n_req, n_tp, bit):
    return [(r * n_tp + t, r * n_tp + (t ^ bit)) for r in range(n_req) for t in range(n_tp)]


def segments(rows):
    e = rows // 4
    return (0, e, 2 * e, 3 * e), (e, e, e, e)


PARTS = {
    "all": (0, 1, 2, 3),
    "half": (0, 1),
    "c": (2,),
    "y": (3,),
}


def shard_index(turn, hops, n_req):
    return hops if turn >= 0 or 2 * hops == n_req else n_req // 2 + hops


def part_rows(part, rows):
    return sum(segments(rows)[1][j] for j in PARTS[part])


def digits(target):
    lane = lax.broadcasted_iota(jnp.int32, (1, LANES), 1)
    shift = jnp.where(lane == 0, 2 * DIGIT_BITS, jnp.where(lane == 1, DIGIT_BITS, 0))
    digit = (target >> shift) & ((1 << DIGIT_BITS) - 1)
    return jnp.where(lane < 3, digit, 0).astype(jnp.float32).astype(jnp.bfloat16)


def undigits(ext):
    lane = lax.broadcasted_iota(jnp.int32, (1, LANES), 1)
    base = float(1 << DIGIT_BITS)
    weight = jnp.where(
        lane == 0, base * base, jnp.where(lane == 1, base, jnp.where(lane == 2, 1.0, 0.0))
    )
    return jnp.sum(ext.astype(jnp.float32) * weight, axis=1, keepdims=True)


def row_stats(logits, target, ids):
    lane = lax.broadcasted_iota(jnp.int32, (1, LANES), 1)
    top = jnp.max(logits, axis=1, keepdims=True)
    shifted = jnp.exp(logits - top)
    weight_sum = jnp.sum(shifted, axis=1, keepdims=True)
    weighted = jnp.sum(shifted * logits, axis=1, keepdims=True)
    width = logits.shape[1] // len(ids)
    hits = [
        jnp.where(part == target, logits[:, k * width : (k + 1) * width], 0.0)
        for k, part in enumerate(ids)
    ]
    picked = jnp.sum(functools.reduce(jnp.add, hits), axis=1, keepdims=True)
    values = jnp.where(lane == 3, picked, 0.0)
    values = jnp.where(lane == 2, weighted, values)
    values = jnp.where(lane == 1, weight_sum, values)
    return jnp.where(lane == 0, top, values)


def vocab_ids(vdev, owner):
    column = lax.broadcasted_iota(jnp.int32, (1, vdev), 1)
    return (column + owner * vdev).astype(jnp.float32)


def norm_kernel(
    n_tp, x_hbm, gain_hbm, tid_hbm, head_hbm, xn_ref, cw_ref, ccw_ref, early_ref,
    x_ref, gain_ref, tid_ref, head_ref, sems,
):
    rows, d = x_ref.shape
    vdev = head_ref.shape[1]
    req, tp = lax.axis_index("req"), lax.axis_index("tp")
    core, plane = tp % 2, tp // 2
    mine = pl.ds(pl.multiple_of(core * rows, rows), rows)
    get_x = pltpu.make_async_copy(x_hbm.at[mine, :], x_ref, sems.at[0])
    get_gain = pltpu.make_async_copy(gain_hbm, gain_ref, sems.at[1])
    get_tid = pltpu.make_async_copy(tid_hbm, tid_ref, sems.at[2])
    get_x.start()
    get_gain.start()
    get_tid.start()
    get_tid.wait()
    target = jnp.where(core == 0, tid_ref[0:1, :], tid_ref[1:2, :])
    target = jnp.broadcast_to(target, (8, rows)).T[:, :1]
    xn_ref[:, d:] = digits(target)
    get_gain.wait()
    get_x.wait()
    feats = x_ref[...].astype(jnp.float32)
    scale = lax.rsqrt(jnp.mean(feats * feats, axis=-1, keepdims=True) + 1e-06)
    xn_ref[:, :d] = (feats * scale * gain_ref[...]).astype(jnp.bfloat16)

    @pl.when(core == 0)
    def _():
        lane = lax.broadcasted_iota(jnp.int32, (rows, LANES), 1)
        early_ref[...] = jnp.where(lane == 0, NOTHING, 0.0)

    @pl.when(core == 1)
    def _():
        get_head = pltpu.make_async_copy(head_hbm, head_ref, sems.at[3])
        get_head.start()
        get_head.wait()
        ids = [vocab_ids(vdev, req * n_tp + tp)]
        k = 0
        for size in EARLY_TILES:
            here = pl.ds(k, size * rows // sum(EARLY_TILES))
            k += here.size
            logits = jnp.dot(xn_ref[here, :d], head_ref[...], preferred_element_type=jnp.float32)
            early_ref[here, :] = row_stats(logits, undigits(xn_ref[here, d:]), ids)

    starts, sizes = segments(rows)
    for ref, flip in ((cw_ref, 0), (ccw_ref, 1)):
        down = plane != flip
        at = 0
        for j in PARTS["half"]:
            start = pl.multiple_of(jnp.where(down, starts[3 - j], starts[j]), 16)
            ref[pl.ds(at, sizes[j]), :] = xn_ref[pl.ds(start, sizes[j]), :]
            at += sizes[j]


def norm_rows(hidden, norm_gain, target_ids, head, n_tp, rows):
    d = hidden.shape[1]
    wide = d + LANES
    message = (part_rows("half", rows), wide)
    hbm_operands = (hidden, norm_gain.reshape(1, d), target_ids.reshape(2, rows), head)
    return pl.pallas_call(
        functools.partial(norm_kernel, n_tp),
        out_shape=[jax.ShapeDtypeStruct(s, jnp.bfloat16) for s in [(rows, wide), message, message]]
        + [jax.ShapeDtypeStruct((rows, LANES), jnp.float32)],
        in_specs=[pl.BlockSpec(memory_space=pl.ANY)] * 4,
        scratch_shapes=[
            pltpu.VMEM((rows, d), jnp.bfloat16),
            pltpu.VMEM((1, d), jnp.float32),
            pltpu.VMEM((2, rows), jnp.int32),
            pltpu.VMEM(head.shape, head.dtype),
            pltpu.SemaphoreType.DMA((4,)),
        ],
        compiler_params=pltpu.CompilerParams(vmem_limit_bytes=VMEM_BYTES),
        name="norm",
    )(*(pltpu.with_memory_space_constraint(v, pltpu.HBM) for v in hbm_operands))


def cut_kernel(plan, n_in, *refs):
    for out_ref, pieces in zip(refs[n_in:], plan):
        to = 0
        for k, at, count in pieces:
            out_ref[pl.ds(to, count), :] = refs[k][pl.ds(at, count), :]
            to += count


def cut(arrays, plan):
    wide = arrays[0].shape[1]
    return pl.pallas_call(
        functools.partial(cut_kernel, plan, len(arrays)),
        out_shape=[
            jax.ShapeDtypeStruct((sum(count for _, _, count in pieces), wide), arrays[0].dtype)
            for pieces in plan
        ],
        compiler_params=pltpu.CompilerParams(vmem_limit_bytes=VMEM_BYTES),
        name="cut",
    )(*arrays)


def stats_kernel(metas, n_req, n_tp, rows, earlier, tail, first, *refs):
    n = len(metas)
    piece_refs, (w0_ref, w1_ref), refs = refs[:n], refs[n : n + 2], refs[n + 2 :]
    if first:
        early_ref, refs = refs[0], refs[1:]
    if tail:
        stat_refs, refs = refs[: len(earlier)], refs[len(earlier) :]
        packed_ref, x_s, l_s, t_s, out_ref = refs
    else:
        out_ref, x_s, l_s, t_s = refs
    req, tp = lax.axis_index("req"), lax.axis_index("tp")
    d, vdev = w0_ref.shape
    total = x_s.shape[0]

    lane = lax.broadcasted_iota(jnp.int32, (1, LANES), 1)
    at = 0
    for parts, ref in zip(metas, piece_refs):
        here = pl.ds(at, ref.shape[0])
        x_s[here, :] = ref[:, :d]
        t_s[here, :] = undigits(ref[:, d:])
        at += ref.shape[0]

    own = tp % 2 == 0 if first else True
    ids = [vocab_ids(vdev, req * n_tp + tp), vocab_ids(vdev, req * n_tp + (tp ^ 1))]
    x = x_s[...]
    l_s[:, vdev:] = jnp.dot(x, w1_ref[...], preferred_element_type=jnp.float32)
    if first:

        @pl.when(own)
        def _():
            l_s[:, :vdev] = jnp.dot(x_s[...], w0_ref[...], preferred_element_type=jnp.float32)

        @pl.when(jnp.logical_not(own))
        def _():
            l_s[:, :vdev] = jnp.full((total, vdev), NOTHING, jnp.float32)

        ids[0] = jnp.where(own, ids[0], -1.0)
    else:
        l_s[:, :vdev] = jnp.dot(x, w0_ref[...], preferred_element_type=jnp.float32)
    step = math.gcd(total, 32)

    def body(i, _):
        here = pl.ds(pl.multiple_of(i * step, step), step)
        out_ref[here, :] = row_stats(l_s[here, :], t_s[here, :], ids)
        return 0

    lax.fori_loop(0, total // step, body, 0, unroll=total // step)
    if first:
        out_ref[...] = merged(out_ref[...], early_ref[...])
    at = 0
    for turn, hops, part in (p for parts in metas for p in parts):
        here = pl.ds(at, part_rows(part, rows))
        at += part_rows(part, rows)
        if hops:
            first = STATS * shard_index(turn, hops, n_req)
            out_ref[here, :] = pltpu.roll(out_ref[here, :], first, 1)
    if tail:
        pack_stats(earlier + (metas,), (*stat_refs, out_ref), packed_ref, n_req, n_tp, rows)


def merged(one, two):
    lane = lax.broadcasted_iota(jnp.int32, (1, LANES), 1)
    top = jnp.maximum(one[:, :1], two[:, :1])
    scaled = one * jnp.exp(one[:, :1] - top) + two * jnp.exp(two[:, :1] - top)
    return jnp.where(lane == 0, top, jnp.where(lane == 3, one + two, scaled))


def pack_stats(metas, stat_refs, packed_ref, n_req, n_tp, rows):
    plane = lax.axis_index("tp") // 2
    place = ring_place(lax.axis_index("req"), n_req)
    _, sizes = segments(rows)
    own, found = None, [[] for _ in sizes]
    for pieces, ref in zip(metas, stat_refs):
        at = 0
        for turn, hops, part in (p for parts in pieces for p in parts):
            for j in PARTS[part]:
                here = ref[pl.ds(at, sizes[j]), :]
                at += sizes[j]
                if hops:
                    found[j if turn > 0 else 3 - j].append(here)
                else:
                    own = ref[...]
    found = [functools.reduce(jnp.add, values) for values in found]
    total = own + jnp.where(
        plane == 0, jnp.concatenate(found, axis=0), jnp.concatenate(found[::-1], axis=0)
    )
    lanes = total.T
    turns = [(0, 0)] + [(1, h) for h in range(1, n_req // 2 + 1)]
    for turn, hops in turns + [(-1, h) for h in range(1, n_req // 2)]:
        source = ring_req((place - turn * hops + n_req) % n_req, n_req)
        k = STATS * shard_index(turn, hops, n_req)
        for t in range(n_tp):
            packed_ref[source * n_tp + t] = lanes[k : k + STATS, :]


def stats_of(
    pieces, metas, w0, w1, n_req, n_tp, rows, early=(), earlier=(), stats=(), tail=False
):
    d, vdev = w0.shape
    total = sum(p.shape[0] for p in pieces)
    row_stats = (total, LANES)
    return pl.pallas_call(
        functools.partial(
            stats_kernel, metas, n_req, n_tp, rows, earlier, tail, len(early) > 0
        ),
        out_shape=jax.ShapeDtypeStruct(
            (n_req * n_tp, STATS, rows) if tail else row_stats, jnp.float32
        ),
        scratch_shapes=[
            pltpu.VMEM((total, d), jnp.bfloat16),
            pltpu.VMEM((total, 2 * vdev), jnp.float32),
            pltpu.VMEM((total, 1), jnp.float32),
        ]
        + [pltpu.VMEM(row_stats, jnp.float32)] * tail,
        compiler_params=pltpu.CompilerParams(vmem_limit_bytes=VMEM_BYTES),
        cost_estimate=pl.CostEstimate(
            flops=4 * total * d * vdev, bytes_accessed=4 * d * vdev, transcendentals=2 * total * vdev
        ),
        name="stats_last" if tail else "stats",
    )(*pieces, w0, w1, *early, *stats)


def final_kernel(n_parts, r_ref, len_ref, lp_ref, ent_ref, mean_ref, top_ref):
    rows = r_ref.shape[2]
    length = len_ref[0]
    total = jnp.float32(0.0)
    best = jnp.float32(-1e30)
    for half in range(2):
        mine = [r_ref[2 * k + half] for k in range(n_parts // 2)]
        top = functools.reduce(jnp.maximum, [m[0:1] for m in mine])
        scaled = functools.reduce(jnp.add, [m * jnp.exp(m[0:1] - top) for m in mine])
        picked = functools.reduce(jnp.add, [m[3:4] for m in mine])
        weight_sum, weighted = scaled[1:2], scaled[2:3]
        log_norm = top + jnp.log(weight_sum)
        slot = lax.broadcasted_iota(jnp.int32, (1, rows), 1) + half * rows
        live = slot < length
        logprob = jnp.where(live, picked - log_norm, 0.0)
        lp_ref[half : half + 1, :] = logprob
        ent_ref[half : half + 1, :] = jnp.where(live, log_norm - weighted / weight_sum, 0.0)
        total += jnp.sum(logprob)
        best = jnp.maximum(best, jnp.max(jnp.where(live, top, -1e30)))
    mean_ref[...] = jnp.full((1, 1), total, jnp.float32) / length.astype(jnp.float32)
    top_ref[...] = jnp.full((1, 1), best, jnp.float32)


def finish(received, lengths):
    n_parts, _, rows = received.shape
    outs = pl.pallas_call(
        functools.partial(final_kernel, n_parts),
        out_shape=[jax.ShapeDtypeStruct((2, rows), jnp.float32)] * 2
        + [jax.ShapeDtypeStruct((1, 1), jnp.float32)] * 2,
        in_specs=[
            pl.BlockSpec(memory_space=pltpu.VMEM),
            pl.BlockSpec(memory_space=pltpu.SMEM),
        ],
        compiler_params=pltpu.CompilerParams(vmem_limit_bytes=VMEM_BYTES),
        name="finish",
    )(received, lengths)
    return tuple(o.reshape(-1) for o in outs)


def per_device(n_req, n_tp, hidden_states, norm_gain, head, target_ids, lengths):
    rows = hidden_states.shape[0] // 2
    cw_pairs, ccw_pairs = ring_pairs(n_req, n_tp, 1), ring_pairs(n_req, n_tp, -1)
    other_core, other_y = tp_pairs(n_req, n_tp, 1), tp_pairs(n_req, n_tp, 2)
    sizes = (n_req, n_tp, rows)
    part = part_rows("y", rows)
    metas, stats = [], []

    def send(value, pairs):
        return lax.ppermute(value, AXES, pairs)

    def work(items, early=()):
        pieces, meta = zip(*items)
        stats.append(stats_of(pieces, meta, head, other_head, *sizes, early=early))
        metas.append(meta)

    def after(value):
        value, stats[-1] = lax.optimization_barrier((value, stats[-1]))
        return value

    other_head = send(head, other_core)
    xn, to_cw, to_ccw, early = norm_rows(
        hidden_states, norm_gain, target_ids, head, n_tp, rows
    )
    items = [(xn, ((0, 0, "all"),))]
    cw, ccw, late = to_cw, to_ccw, []
    for hops in range(1, n_req // 2 + 1):
        next_cw, next_ccw = send(cw, cw_pairs), send(ccw, ccw_pairs)
        others = []
        both = [(0, 0, part), (1, 0, part)]
        if hops == 2:
            (c_both,) = cut((cw, ccw), [[(0, part, part), (1, part, part)]])
            c_both = send(c_both, other_y)
            others = [(c_both, ((1, 1, "c"), (-1, 1, "c")))]
        elif hops > 2:
            (y_message,) = cut((cw, ccw), [both])
            y_next = send(y_message, other_y)
            if hops == 3:
                c_cw, c_ccw = cut((c_both,), [[both[0]], [(0, part, part)]])
            else:
                c_cw, c_ccw, _ = lax.optimization_barrier((c_cw, c_ccw, y_message))
            c_cw, c_ccw = send(c_cw, cw_pairs), send(c_ccw, ccw_pairs)
            others = late + [
                (c_cw, ((1, hops - 1, "c"),)),
                (c_ccw, ((-1, hops - 1, "c"),)),
                (y_next, ((1, hops - 1, "y"), (-1, hops - 1, "y"))),
            ]
            late = []
        work(items, () if stats else (early,))
        if hops == 2:
            (y_message,) = cut((cw, ccw), [both])
            late = [(send(y_message, other_y), ((1, 1, "y"), (-1, 1, "y")))]
        cw, ccw = after(next_cw), after(next_ccw)
        items = [(cw, ((1, hops, "half"),)), (ccw, ((-1, hops, "half"),))]
        if 2 * hops == n_req:
            work(items)
            items = []
        items += others
        if hops == 2:
            items, late = items + late, []
    pieces, meta = zip(*items)
    packed = stats_of(
        pieces, meta, head, other_head, *sizes, earlier=tuple(metas), stats=stats, tail=True
    )
    received = lax.all_to_all(packed, AXES, 0, 0, tiled=True)
    return finish(received, lengths)


def solution(mesh):
    n_req, n_tp = mesh.shape["req"], mesh.shape["tp"]
    in_specs = (P("req", None), P(), P(None, ("req", "tp")), P("req"), P("req"))
    out_specs = (P("req"), P("req"), P("req"), P("req"))
    return jax.shard_map(
        functools.partial(per_device, n_req, n_tp),
        mesh=mesh,
        in_specs=in_specs,
        out_specs=out_specs,
        check_vma=False,
    )
```

```python
import functools
import math

import jax
import jax.numpy as jnp
from jax import lax
from jax.experimental import pallas as pl
from jax.experimental.pallas import tpu as pltpu
from jax.sharding import PartitionSpec as P

AXES = ("req", "tp")
LANES = 128
STATS = 4
DIGIT_BITS = 7
NOTHING = -1e30
EARLY_TILES = (32, 32, 16, 16, 16, 16)
VMEM_BYTES = 10 * 1024 * 1024


def ring_place(req, n_req):
    half = n_req // 2
    return jnp.where(req % 2 == 0, req // 2, n_req - 1 - req // 2) if half else req


def ring_req(place, n_req):
    half = n_req // 2
    return jnp.where(place < half, 2 * place, 2 * (n_req - 1 - place) + 1)


def ring_req_py(place, n_req):
    place %= n_req
    return 2 * place if place < n_req // 2 else 2 * (n_req - 1 - place) + 1


def ring_pairs(n_req, n_tp, turn):
    pairs = []
    for place in range(n_req):
        here, there = ring_req_py(place, n_req), ring_req_py(place + turn, n_req)
        pairs += [(here * n_tp + t, there * n_tp + t) for t in range(n_tp)]
    return pairs


def tp_pairs(n_req, n_tp, bit):
    return [(r * n_tp + t, r * n_tp + (t ^ bit)) for r in range(n_req) for t in range(n_tp)]


def segments(rows):
    e = rows // 4
    return (0, e, 2 * e, 3 * e), (e, e, e, e)


PARTS = {
    "all": (0, 1, 2, 3),
    "half": (0, 1),
    "c": (2,),
    "y": (3,),
}


def shard_index(turn, hops, n_req):
    return hops if turn >= 0 or 2 * hops == n_req else n_req // 2 + hops


def part_rows(part, rows):
    return sum(segments(rows)[1][j] for j in PARTS[part])


def digits(target):
    lane = lax.broadcasted_iota(jnp.int32, (1, LANES), 1)
    shift = jnp.where(lane == 0, 2 * DIGIT_BITS, jnp.where(lane == 1, DIGIT_BITS, 0))
    digit = (target >> shift) & ((1 << DIGIT_BITS) - 1)
    return jnp.where(lane < 3, digit, 0).astype(jnp.float32).astype(jnp.bfloat16)


def undigits(ext):
    lane = lax.broadcasted_iota(jnp.int32, (1, LANES), 1)
    base = float(1 << DIGIT_BITS)
    weight = jnp.where(
        lane == 0, base * base, jnp.where(lane == 1, base, jnp.where(lane == 2, 1.0, 0.0))
    )
    return jnp.sum(ext.astype(jnp.float32) * weight, axis=1, keepdims=True)


def row_stats(logits, target, ids):
    lane = lax.broadcasted_iota(jnp.int32, (1, LANES), 1)
    top = jnp.max(logits, axis=1, keepdims=True)
    shifted = jnp.exp(logits - top)
    weight_sum = jnp.sum(shifted, axis=1, keepdims=True)
    weighted = jnp.sum(shifted * logits, axis=1, keepdims=True)
    width = logits.shape[1] // len(ids)
    hits = [
        jnp.where(part == target, logits[:, k * width : (k + 1) * width], 0.0)
        for k, part in enumerate(ids)
    ]
    picked = jnp.sum(functools.reduce(jnp.add, hits), axis=1, keepdims=True)
    values = jnp.where(lane == 3, picked, 0.0)
    values = jnp.where(lane == 2, weighted, values)
    values = jnp.where(lane == 1, weight_sum, values)
    return jnp.where(lane == 0, top, values)


def vocab_ids(vdev, owner):
    column = lax.broadcasted_iota(jnp.int32, (1, vdev), 1)
    return (column + owner * vdev).astype(jnp.float32)


def norm_kernel(
    n_tp, x_hbm, gain_hbm, tid_hbm, head_hbm, xn_ref, cw_ref, ccw_ref, early_ref,
    x_ref, gain_ref, tid_ref, head_ref, sems,
):
    rows, d = x_ref.shape
    vdev = head_ref.shape[1]
    req, tp = lax.axis_index("req"), lax.axis_index("tp")
    core, plane = tp % 2, tp // 2
    mine = pl.ds(pl.multiple_of(core * rows, rows), rows)
    get_x = pltpu.make_async_copy(x_hbm.at[mine, :], x_ref, sems.at[0])
    get_gain = pltpu.make_async_copy(gain_hbm, gain_ref, sems.at[1])
    get_tid = pltpu.make_async_copy(tid_hbm, tid_ref, sems.at[2])
    get_x.start()
    get_gain.start()
    get_tid.start()
    get_tid.wait()
    target = jnp.where(core == 0, tid_ref[0:1, :], tid_ref[1:2, :])
    target = jnp.broadcast_to(target, (8, rows)).T[:, :1]
    xn_ref[:, d:] = digits(target)
    get_gain.wait()
    get_x.wait()
    feats = x_ref[...].astype(jnp.float32)
    scale = lax.rsqrt(jnp.mean(feats * feats, axis=-1, keepdims=True) + 1e-06)
    xn_ref[:, :d] = (feats * scale * gain_ref[...]).astype(jnp.bfloat16)

    @pl.when(core == 1)
    def _():
        get_head = pltpu.make_async_copy(head_hbm, head_ref, sems.at[3])
        get_head.start()
        get_head.wait()
        ids = [vocab_ids(vdev, req * n_tp + tp)]
        k = 0
        for size in EARLY_TILES:
            here = pl.ds(k, size * rows // sum(EARLY_TILES))
            k += here.size
            logits = jnp.dot(xn_ref[here, :d], head_ref[...], preferred_element_type=jnp.float32)
            early_ref[here, :] = row_stats(logits, undigits(xn_ref[here, d:]), ids)

    starts, sizes = segments(rows)
    for ref, flip in ((cw_ref, 0), (ccw_ref, 1)):
        down = plane != flip
        at = 0
        for j in PARTS["half"]:
            start = pl.multiple_of(jnp.where(down, starts[3 - j], starts[j]), 16)
            ref[pl.ds(at, sizes[j]), :] = xn_ref[pl.ds(start, sizes[j]), :]
            at += sizes[j]


def norm_rows(hidden, norm_gain, target_ids, head, n_tp, rows):
    d = hidden.shape[1]
    wide = d + LANES
    message = (part_rows("half", rows), wide)
    hbm_operands = (hidden, norm_gain.reshape(1, d), target_ids.reshape(2, rows), head)
    return pl.pallas_call(
        functools.partial(norm_kernel, n_tp),
        out_shape=[jax.ShapeDtypeStruct(s, jnp.bfloat16) for s in [(rows, wide), message, message]]
        + [jax.ShapeDtypeStruct((rows, LANES), jnp.float32)],
        in_specs=[pl.BlockSpec(memory_space=pl.ANY)] * 4,
        scratch_shapes=[
            pltpu.VMEM((rows, d), jnp.bfloat16),
            pltpu.VMEM((1, d), jnp.float32),
            pltpu.VMEM((2, rows), jnp.int32),
            pltpu.VMEM(head.shape, head.dtype),
            pltpu.SemaphoreType.DMA((4,)),
        ],
        compiler_params=pltpu.CompilerParams(vmem_limit_bytes=VMEM_BYTES),
        name="norm",
    )(*(pltpu.with_memory_space_constraint(v, pltpu.HBM) for v in hbm_operands))


def cut_kernel(plan, n_in, *refs):
    for out_ref, pieces in zip(refs[n_in:], plan):
        to = 0
        for k, at, count in pieces:
            out_ref[pl.ds(to, count), :] = refs[k][pl.ds(at, count), :]
            to += count


def cut(arrays, plan):
    wide = arrays[0].shape[1]
    return pl.pallas_call(
        functools.partial(cut_kernel, plan, len(arrays)),
        out_shape=[
            jax.ShapeDtypeStruct((sum(count for _, _, count in pieces), wide), arrays[0].dtype)
            for pieces in plan
        ],
        compiler_params=pltpu.CompilerParams(vmem_limit_bytes=VMEM_BYTES),
        name="cut",
    )(*arrays)


def stats_kernel(metas, n_req, n_tp, rows, earlier, tail, first, *refs):
    n = len(metas)
    piece_refs, (w0_ref, w1_ref), refs = refs[:n], refs[n : n + 2], refs[n + 2 :]
    if first:
        early_ref, refs = refs[0], refs[1:]
    if tail:
        stat_refs, refs = refs[: len(earlier)], refs[len(earlier) :]
        packed_ref, x_s, l_s, t_s, out_ref = refs
    else:
        out_ref, x_s, l_s, t_s = refs
    req, tp = lax.axis_index("req"), lax.axis_index("tp")
    d, vdev = w0_ref.shape
    total = x_s.shape[0]

    lane = lax.broadcasted_iota(jnp.int32, (1, LANES), 1)
    at = 0
    for parts, ref in zip(metas, piece_refs):
        here = pl.ds(at, ref.shape[0])
        x_s[here, :] = ref[:, :d]
        t_s[here, :] = undigits(ref[:, d:])
        at += ref.shape[0]

    own = tp % 2 == 0 if first else True
    ids = [vocab_ids(vdev, req * n_tp + tp), vocab_ids(vdev, req * n_tp + (tp ^ 1))]
    x = x_s[...]
    l_s[:, vdev:] = jnp.dot(x, w1_ref[...], preferred_element_type=jnp.float32)
    if first:

        @pl.when(own)
        def _():
            l_s[:, :vdev] = jnp.dot(x_s[...], w0_ref[...], preferred_element_type=jnp.float32)

        @pl.when(jnp.logical_not(own))
        def _():
            l_s[:, :vdev] = jnp.full((total, vdev), NOTHING, jnp.float32)

        ids[0] = jnp.where(own, ids[0], -1.0)
    else:
        l_s[:, :vdev] = jnp.dot(x, w0_ref[...], preferred_element_type=jnp.float32)
    step = math.gcd(total, 32)

    def body(i, _):
        here = pl.ds(pl.multiple_of(i * step, step), step)
        out_ref[here, :] = row_stats(l_s[here, :], t_s[here, :], ids)
        return 0

    lax.fori_loop(0, total // step, body, 0, unroll=total // step)
    if first:

        @pl.when(jnp.logical_not(own))
        def _():
            out_ref[...] = merged(out_ref[...], early_ref[...])

    at = 0
    for turn, hops, part in (p for parts in metas for p in parts):
        here = pl.ds(at, part_rows(part, rows))
        at += part_rows(part, rows)
        if hops:
            first = STATS * shard_index(turn, hops, n_req)
            out_ref[here, :] = pltpu.roll(out_ref[here, :], first, 1)
    if tail:
        pack_stats(earlier + (metas,), (*stat_refs, out_ref), packed_ref, n_req, n_tp, rows)


def merged(one, two):
    lane = lax.broadcasted_iota(jnp.int32, (1, LANES), 1)
    top = jnp.maximum(one[:, :1], two[:, :1])
    scaled = one * jnp.exp(one[:, :1] - top) + two * jnp.exp(two[:, :1] - top)
    return jnp.where(lane == 0, top, jnp.where(lane == 3, one + two, scaled))


def pack_stats(metas, stat_refs, packed_ref, n_req, n_tp, rows):
    plane = lax.axis_index("tp") // 2
    place = ring_place(lax.axis_index("req"), n_req)
    _, sizes = segments(rows)
    own, found = None, [[] for _ in sizes]
    for pieces, ref in zip(metas, stat_refs):
        at = 0
        for turn, hops, part in (p for parts in pieces for p in parts):
            for j in PARTS[part]:
                here = ref[pl.ds(at, sizes[j]), :]
                at += sizes[j]
                if hops:
                    found[j if turn > 0 else 3 - j].append(here)
                else:
                    own = ref[...]
    found = [functools.reduce(jnp.add, values) for values in found]
    total = own + jnp.where(
        plane == 0, jnp.concatenate(found, axis=0), jnp.concatenate(found[::-1], axis=0)
    )
    lanes = total.T
    turns = [(0, 0)] + [(1, h) for h in range(1, n_req // 2 + 1)]
    for turn, hops in turns + [(-1, h) for h in range(1, n_req // 2)]:
        source = ring_req((place - turn * hops + n_req) % n_req, n_req)
        k = STATS * shard_index(turn, hops, n_req)
        for t in range(n_tp):
            packed_ref[source * n_tp + t] = lanes[k : k + STATS, :]


def stats_of(
    pieces, metas, w0, w1, n_req, n_tp, rows, early=(), earlier=(), stats=(), tail=False
):
    d, vdev = w0.shape
    total = sum(p.shape[0] for p in pieces)
    row_stats = (total, LANES)
    return pl.pallas_call(
        functools.partial(
            stats_kernel, metas, n_req, n_tp, rows, earlier, tail, len(early) > 0
        ),
        out_shape=jax.ShapeDtypeStruct(
            (n_req * n_tp, STATS, rows) if tail else row_stats, jnp.float32
        ),
        scratch_shapes=[
            pltpu.VMEM((total, d), jnp.bfloat16),
            pltpu.VMEM((total, 2 * vdev), jnp.float32),
            pltpu.VMEM((total, 1), jnp.float32),
        ]
        + [pltpu.VMEM(row_stats, jnp.float32)] * tail,
        compiler_params=pltpu.CompilerParams(vmem_limit_bytes=VMEM_BYTES),
        cost_estimate=pl.CostEstimate(
            flops=4 * total * d * vdev, bytes_accessed=4 * d * vdev, transcendentals=2 * total * vdev
        ),
        name="stats_last" if tail else "stats",
    )(*pieces, w0, w1, *early, *stats)


def final_kernel(n_parts, r_ref, len_ref, lp_ref, ent_ref, mean_ref, top_ref):
    rows = r_ref.shape[2]
    length = len_ref[0]
    total = jnp.float32(0.0)
    best = jnp.float32(-1e30)
    for half in range(2):
        mine = [r_ref[2 * k + half] for k in range(n_parts // 2)]
        top = functools.reduce(jnp.maximum, [m[0:1] for m in mine])
        scaled = functools.reduce(jnp.add, [m * jnp.exp(m[0:1] - top) for m in mine])
        picked = functools.reduce(jnp.add, [m[3:4] for m in mine])
        weight_sum, weighted = scaled[1:2], scaled[2:3]
        log_norm = top + jnp.log(weight_sum)
        slot = lax.broadcasted_iota(jnp.int32, (1, rows), 1) + half * rows
        live = slot < length
        logprob = jnp.where(live, picked - log_norm, 0.0)
        lp_ref[half : half + 1, :] = logprob
        ent_ref[half : half + 1, :] = jnp.where(live, log_norm - weighted / weight_sum, 0.0)
        total += jnp.sum(logprob)
        best = jnp.maximum(best, jnp.max(jnp.where(live, top, -1e30)))
    mean_ref[...] = jnp.full((1, 1), total, jnp.float32) / length.astype(jnp.float32)
    top_ref[...] = jnp.full((1, 1), best, jnp.float32)


def finish(received, lengths):
    n_parts, _, rows = received.shape
    outs = pl.pallas_call(
        functools.partial(final_kernel, n_parts),
        out_shape=[jax.ShapeDtypeStruct((2, rows), jnp.float32)] * 2
        + [jax.ShapeDtypeStruct((1, 1), jnp.float32)] * 2,
        in_specs=[
            pl.BlockSpec(memory_space=pltpu.VMEM),
            pl.BlockSpec(memory_space=pltpu.SMEM),
        ],
        compiler_params=pltpu.CompilerParams(vmem_limit_bytes=VMEM_BYTES),
        name="finish",
    )(received, lengths)
    return tuple(o.reshape(-1) for o in outs)


def per_device(n_req, n_tp, hidden_states, norm_gain, head, target_ids, lengths):
    rows = hidden_states.shape[0] // 2
    cw_pairs, ccw_pairs = ring_pairs(n_req, n_tp, 1), ring_pairs(n_req, n_tp, -1)
    other_core, other_y = tp_pairs(n_req, n_tp, 1), tp_pairs(n_req, n_tp, 2)
    sizes = (n_req, n_tp, rows)
    part = part_rows("y", rows)
    metas, stats = [], []

    def send(value, pairs):
        return lax.ppermute(value, AXES, pairs)

    def work(items, early=()):
        pieces, meta = zip(*items)
        stats.append(stats_of(pieces, meta, head, other_head, *sizes, early=early))
        metas.append(meta)

    def after(value):
        value, stats[-1] = lax.optimization_barrier((value, stats[-1]))
        return value

    other_head = send(head, other_core)
    xn, to_cw, to_ccw, early = norm_rows(
        hidden_states, norm_gain, target_ids, head, n_tp, rows
    )
    items = [(xn, ((0, 0, "all"),))]
    cw, ccw, late = to_cw, to_ccw, []
    for hops in range(1, n_req // 2 + 1):
        next_cw, next_ccw = send(cw, cw_pairs), send(ccw, ccw_pairs)
        others = []
        both = [(0, 0, part), (1, 0, part)]
        if hops == 2:
            (c_both,) = cut((cw, ccw), [[(0, part, part), (1, part, part)]])
            c_both = send(c_both, other_y)
            others = [(c_both, ((1, 1, "c"), (-1, 1, "c")))]
        elif hops > 2:
            (y_message,) = cut((cw, ccw), [both])
            y_next = send(y_message, other_y)
            if hops == 3:
                c_cw, c_ccw = cut((c_both,), [[both[0]], [(0, part, part)]])
            else:
                c_cw, c_ccw, _ = lax.optimization_barrier((c_cw, c_ccw, y_message))
            c_cw, c_ccw = send(c_cw, cw_pairs), send(c_ccw, ccw_pairs)
            others = late + [
                (c_cw, ((1, hops - 1, "c"),)),
                (c_ccw, ((-1, hops - 1, "c"),)),
                (y_next, ((1, hops - 1, "y"), (-1, hops - 1, "y"))),
            ]
            late = []
        work(items, () if stats else (early,))
        if hops == 2:
            (y_message,) = cut((cw, ccw), [both])
            late = [(send(y_message, other_y), ((1, 1, "y"), (-1, 1, "y")))]
        cw, ccw = after(next_cw), after(next_ccw)
        items = [(cw, ((1, hops, "half"),)), (ccw, ((-1, hops, "half"),))]
        if 2 * hops == n_req:
            work(items)
            items = []
        items += others
        if hops == 2:
            items, late = items + late, []
    pieces, meta = zip(*items)
    packed = stats_of(
        pieces, meta, head, other_head, *sizes, earlier=tuple(metas), stats=stats, tail=True
    )
    received = lax.all_to_all(packed, AXES, 0, 0, tiled=True)
    return finish(received, lengths)


def solution(mesh):
    n_req, n_tp = mesh.shape["req"], mesh.shape["tp"]
    in_specs = (P("req", None), P(), P(None, ("req", "tp")), P("req"), P("req"))
    out_specs = (P("req"), P("req"), P("req"), P("req"))
    return jax.shard_map(
        functools.partial(per_device, n_req, n_tp),
        mesh=mesh,
        in_specs=in_specs,
        out_specs=out_specs,
        check_vma=False,
    )
```

```python
import functools
import math

import jax
import jax.numpy as jnp
from jax import lax
from jax.experimental import pallas as pl
from jax.experimental.pallas import tpu as pltpu
from jax.sharding import PartitionSpec as P

AXES = ("req", "tp")
LANES = 128
STATS = 4
DIGIT_BITS = 7
NOTHING = -1e30
EARLY_TILES = ((32, 16, 16, 16, 16, 16, 16), (32, 32, 16, 16, 16, 16))
VMEM_BYTES = 10 * 1024 * 1024


def ring_place(req, n_req):
    half = n_req // 2
    return jnp.where(req % 2 == 0, req // 2, n_req - 1 - req // 2) if half else req


def ring_req(place, n_req):
    half = n_req // 2
    return jnp.where(place < half, 2 * place, 2 * (n_req - 1 - place) + 1)


def ring_req_py(place, n_req):
    place %= n_req
    return 2 * place if place < n_req // 2 else 2 * (n_req - 1 - place) + 1


def ring_pairs(n_req, n_tp, turn):
    pairs = []
    for place in range(n_req):
        here, there = ring_req_py(place, n_req), ring_req_py(place + turn, n_req)
        pairs += [(here * n_tp + t, there * n_tp + t) for t in range(n_tp)]
    return pairs


def tp_pairs(n_req, n_tp, bit):
    return [(r * n_tp + t, r * n_tp + (t ^ bit)) for r in range(n_req) for t in range(n_tp)]


def segments(rows):
    e = rows // 4
    return (0, e, 2 * e, 3 * e), (e, e, e, e)


PARTS = {
    "all": (0, 1, 2, 3),
    "half": (0, 1),
    "c": (2,),
    "y": (3,),
}


def shard_index(turn, hops, n_req):
    return hops if turn >= 0 or 2 * hops == n_req else n_req // 2 + hops


def part_rows(part, rows):
    return sum(segments(rows)[1][j] for j in PARTS[part])


def digits(target):
    lane = lax.broadcasted_iota(jnp.int32, (1, LANES), 1)
    shift = jnp.where(lane == 0, 2 * DIGIT_BITS, jnp.where(lane == 1, DIGIT_BITS, 0))
    digit = (target >> shift) & ((1 << DIGIT_BITS) - 1)
    return jnp.where(lane < 3, digit, 0).astype(jnp.float32).astype(jnp.bfloat16)


def undigits(ext):
    lane = lax.broadcasted_iota(jnp.int32, (1, LANES), 1)
    base = float(1 << DIGIT_BITS)
    weight = jnp.where(
        lane == 0, base * base, jnp.where(lane == 1, base, jnp.where(lane == 2, 1.0, 0.0))
    )
    return jnp.sum(ext.astype(jnp.float32) * weight, axis=1, keepdims=True)


def row_stats(logits, target, ids):
    lane = lax.broadcasted_iota(jnp.int32, (1, LANES), 1)
    top = jnp.max(logits, axis=1, keepdims=True)
    shifted = jnp.exp(logits - top)
    weight_sum = jnp.sum(shifted, axis=1, keepdims=True)
    weighted = jnp.sum(shifted * logits, axis=1, keepdims=True)
    width = logits.shape[1] // len(ids)
    hits = [
        jnp.where(part == target, logits[:, k * width : (k + 1) * width], 0.0)
        for k, part in enumerate(ids)
    ]
    picked = jnp.sum(functools.reduce(jnp.add, hits), axis=1, keepdims=True)
    values = jnp.where(lane == 3, picked, 0.0)
    values = jnp.where(lane == 2, weighted, values)
    values = jnp.where(lane == 1, weight_sum, values)
    return jnp.where(lane == 0, top, values)


def vocab_ids(vdev, owner):
    column = lax.broadcasted_iota(jnp.int32, (1, vdev), 1)
    return (column + owner * vdev).astype(jnp.float32)


def norm_kernel(
    n_tp, x_hbm, gain_hbm, tid_hbm, head_hbm, xn_ref, cw_ref, ccw_ref, early_ref,
    x_ref, gain_ref, tid_ref, head_ref, sems,
):
    rows, d = x_ref.shape
    vdev = head_ref.shape[1]
    req, tp = lax.axis_index("req"), lax.axis_index("tp")
    core, plane = tp % 2, tp // 2
    mine = pl.ds(pl.multiple_of(core * rows, rows), rows)
    get_x = pltpu.make_async_copy(x_hbm.at[mine, :], x_ref, sems.at[0])
    get_gain = pltpu.make_async_copy(gain_hbm, gain_ref, sems.at[1])
    get_tid = pltpu.make_async_copy(tid_hbm, tid_ref, sems.at[2])
    get_x.start()
    get_gain.start()
    get_tid.start()
    get_tid.wait()
    target = jnp.where(core == 0, tid_ref[0:1, :], tid_ref[1:2, :])
    target = jnp.broadcast_to(target, (8, rows)).T[:, :1]
    xn_ref[:, d:] = digits(target)
    get_gain.wait()
    get_x.wait()
    feats = x_ref[...].astype(jnp.float32)
    scale = lax.rsqrt(jnp.mean(feats * feats, axis=-1, keepdims=True) + 1e-06)
    xn_ref[:, :d] = (feats * scale * gain_ref[...]).astype(jnp.bfloat16)

    @pl.when(core == 0)
    def _():
        lane = lax.broadcasted_iota(jnp.int32, (rows, LANES), 1)
        early_ref[...] = jnp.where(lane == 0, NOTHING, 0.0)

    def early(tiles):
        get_head = pltpu.make_async_copy(head_hbm, head_ref, sems.at[3])
        get_head.start()
        get_head.wait()
        ids = [vocab_ids(vdev, req * n_tp + tp)]
        k = 0
        for size in tiles:
            here = pl.ds(k, size * rows // sum(tiles))
            k += here.size
            logits = jnp.dot(xn_ref[here, :d], head_ref[...], preferred_element_type=jnp.float32)
            early_ref[here, :] = row_stats(logits, undigits(xn_ref[here, d:]), ids)

    for own_plane, tiles in enumerate(EARLY_TILES):
        pl.when((core == 1) & (plane == own_plane))(functools.partial(early, tiles))

    starts, sizes = segments(rows)
    for ref, flip in ((cw_ref, 0), (ccw_ref, 1)):
        down = plane != flip
        at = 0
        for j in PARTS["half"]:
            start = pl.multiple_of(jnp.where(down, starts[3 - j], starts[j]), 16)
            ref[pl.ds(at, sizes[j]), :] = xn_ref[pl.ds(start, sizes[j]), :]
            at += sizes[j]


def norm_rows(hidden, norm_gain, target_ids, head, n_tp, rows):
    d = hidden.shape[1]
    wide = d + LANES
    message = (part_rows("half", rows), wide)
    hbm_operands = (hidden, norm_gain.reshape(1, d), target_ids.reshape(2, rows), head)
    return pl.pallas_call(
        functools.partial(norm_kernel, n_tp),
        out_shape=[jax.ShapeDtypeStruct(s, jnp.bfloat16) for s in [(rows, wide), message, message]]
        + [jax.ShapeDtypeStruct((rows, LANES), jnp.float32)],
        in_specs=[pl.BlockSpec(memory_space=pl.ANY)] * 4,
        scratch_shapes=[
            pltpu.VMEM((rows, d), jnp.bfloat16),
            pltpu.VMEM((1, d), jnp.float32),
            pltpu.VMEM((2, rows), jnp.int32),
            pltpu.VMEM(head.shape, head.dtype),
            pltpu.SemaphoreType.DMA((4,)),
        ],
        compiler_params=pltpu.CompilerParams(vmem_limit_bytes=VMEM_BYTES),
        name="norm",
    )(*(pltpu.with_memory_space_constraint(v, pltpu.HBM) for v in hbm_operands))


def cut_kernel(plan, n_in, *refs):
    for out_ref, pieces in zip(refs[n_in:], plan):
        to = 0
        for k, at, count in pieces:
            out_ref[pl.ds(to, count), :] = refs[k][pl.ds(at, count), :]
            to += count


def cut(arrays, plan):
    wide = arrays[0].shape[1]
    return pl.pallas_call(
        functools.partial(cut_kernel, plan, len(arrays)),
        out_shape=[
            jax.ShapeDtypeStruct((sum(count for _, _, count in pieces), wide), arrays[0].dtype)
            for pieces in plan
        ],
        compiler_params=pltpu.CompilerParams(vmem_limit_bytes=VMEM_BYTES),
        name="cut",
    )(*arrays)


def stats_kernel(metas, n_req, n_tp, rows, earlier, tail, first, *refs):
    n = len(metas)
    piece_refs, (w0_ref, w1_ref), refs = refs[:n], refs[n : n + 2], refs[n + 2 :]
    if first:
        early_ref, refs = refs[0], refs[1:]
    if tail:
        stat_refs, refs = refs[: len(earlier)], refs[len(earlier) :]
        packed_ref, x_s, l_s, t_s, out_ref = refs
    else:
        out_ref, x_s, l_s, t_s = refs
    req, tp = lax.axis_index("req"), lax.axis_index("tp")
    d, vdev = w0_ref.shape
    total = x_s.shape[0]

    lane = lax.broadcasted_iota(jnp.int32, (1, LANES), 1)
    at = 0
    for parts, ref in zip(metas, piece_refs):
        here = pl.ds(at, ref.shape[0])
        x_s[here, :] = ref[:, :d]
        t_s[here, :] = undigits(ref[:, d:])
        at += ref.shape[0]

    own = tp % 2 == 0 if first else True
    ids = [vocab_ids(vdev, req * n_tp + tp), vocab_ids(vdev, req * n_tp + (tp ^ 1))]
    x = x_s[...]
    l_s[:, vdev:] = jnp.dot(x, w1_ref[...], preferred_element_type=jnp.float32)
    if first:

        @pl.when(own)
        def _():
            l_s[:, :vdev] = jnp.dot(x_s[...], w0_ref[...], preferred_element_type=jnp.float32)

        @pl.when(jnp.logical_not(own))
        def _():
            l_s[:, :vdev] = jnp.full((total, vdev), NOTHING, jnp.float32)

        ids[0] = jnp.where(own, ids[0], -1.0)
    else:
        l_s[:, :vdev] = jnp.dot(x, w0_ref[...], preferred_element_type=jnp.float32)
    step = math.gcd(total, 32)

    def body(i, _):
        here = pl.ds(pl.multiple_of(i * step, step), step)
        out_ref[here, :] = row_stats(l_s[here, :], t_s[here, :], ids)
        return 0

    lax.fori_loop(0, total // step, body, 0, unroll=total // step)
    if first:
        out_ref[...] = merged(out_ref[...], early_ref[...])
    at = 0
    for turn, hops, part in (p for parts in metas for p in parts):
        here = pl.ds(at, part_rows(part, rows))
        at += part_rows(part, rows)
        if hops:
            first = STATS * shard_index(turn, hops, n_req)
            out_ref[here, :] = pltpu.roll(out_ref[here, :], first, 1)
    if tail:
        pack_stats(earlier + (metas,), (*stat_refs, out_ref), packed_ref, n_req, n_tp, rows)


def merged(one, two):
    lane = lax.broadcasted_iota(jnp.int32, (1, LANES), 1)
    top = jnp.maximum(one[:, :1], two[:, :1])
    scaled = one * jnp.exp(one[:, :1] - top) + two * jnp.exp(two[:, :1] - top)
    return jnp.where(lane == 0, top, jnp.where(lane == 3, one + two, scaled))


def pack_stats(metas, stat_refs, packed_ref, n_req, n_tp, rows):
    plane = lax.axis_index("tp") // 2
    place = ring_place(lax.axis_index("req"), n_req)
    _, sizes = segments(rows)
    own, found = None, [[] for _ in sizes]
    for pieces, ref in zip(metas, stat_refs):
        at = 0
        for turn, hops, part in (p for parts in pieces for p in parts):
            for j in PARTS[part]:
                here = ref[pl.ds(at, sizes[j]), :]
                at += sizes[j]
                if hops:
                    found[j if turn > 0 else 3 - j].append(here)
                else:
                    own = ref[...]
    found = [functools.reduce(jnp.add, values) for values in found]
    total = own + jnp.where(
        plane == 0, jnp.concatenate(found, axis=0), jnp.concatenate(found[::-1], axis=0)
    )
    lanes = total.T
    turns = [(0, 0)] + [(1, h) for h in range(1, n_req // 2 + 1)]
    for turn, hops in turns + [(-1, h) for h in range(1, n_req // 2)]:
        source = ring_req((place - turn * hops + n_req) % n_req, n_req)
        k = STATS * shard_index(turn, hops, n_req)
        for t in range(n_tp):
            packed_ref[source * n_tp + t] = lanes[k : k + STATS, :]


def stats_of(
    pieces, metas, w0, w1, n_req, n_tp, rows, early=(), earlier=(), stats=(), tail=False
):
    d, vdev = w0.shape
    total = sum(p.shape[0] for p in pieces)
    row_stats = (total, LANES)
    return pl.pallas_call(
        functools.partial(
            stats_kernel, metas, n_req, n_tp, rows, earlier, tail, len(early) > 0
        ),
        out_shape=jax.ShapeDtypeStruct(
            (n_req * n_tp, STATS, rows) if tail else row_stats, jnp.float32
        ),
        scratch_shapes=[
            pltpu.VMEM((total, d), jnp.bfloat16),
            pltpu.VMEM((total, 2 * vdev), jnp.float32),
            pltpu.VMEM((total, 1), jnp.float32),
        ]
        + [pltpu.VMEM(row_stats, jnp.float32)] * tail,
        compiler_params=pltpu.CompilerParams(vmem_limit_bytes=VMEM_BYTES),
        cost_estimate=pl.CostEstimate(
            flops=4 * total * d * vdev, bytes_accessed=4 * d * vdev, transcendentals=2 * total * vdev
        ),
        name="stats_last" if tail else "stats",
    )(*pieces, w0, w1, *early, *stats)


def final_kernel(n_parts, r_ref, len_ref, lp_ref, ent_ref, mean_ref, top_ref):
    rows = r_ref.shape[2]
    length = len_ref[0]
    total = jnp.float32(0.0)
    best = jnp.float32(-1e30)
    for half in range(2):
        mine = [r_ref[2 * k + half] for k in range(n_parts // 2)]
        top = functools.reduce(jnp.maximum, [m[0:1] for m in mine])
        scaled = functools.reduce(jnp.add, [m * jnp.exp(m[0:1] - top) for m in mine])
        picked = functools.reduce(jnp.add, [m[3:4] for m in mine])
        weight_sum, weighted = scaled[1:2], scaled[2:3]
        log_norm = top + jnp.log(weight_sum)
        slot = lax.broadcasted_iota(jnp.int32, (1, rows), 1) + half * rows
        live = slot < length
        logprob = jnp.where(live, picked - log_norm, 0.0)
        lp_ref[half : half + 1, :] = logprob
        ent_ref[half : half + 1, :] = jnp.where(live, log_norm - weighted / weight_sum, 0.0)
        total += jnp.sum(logprob)
        best = jnp.maximum(best, jnp.max(jnp.where(live, top, -1e30)))
    mean_ref[...] = jnp.full((1, 1), total, jnp.float32) / length.astype(jnp.float32)
    top_ref[...] = jnp.full((1, 1), best, jnp.float32)


def finish(received, lengths):
    n_parts, _, rows = received.shape
    outs = pl.pallas_call(
        functools.partial(final_kernel, n_parts),
        out_shape=[jax.ShapeDtypeStruct((2, rows), jnp.float32)] * 2
        + [jax.ShapeDtypeStruct((1, 1), jnp.float32)] * 2,
        in_specs=[
            pl.BlockSpec(memory_space=pltpu.VMEM),
            pl.BlockSpec(memory_space=pltpu.SMEM),
        ],
        compiler_params=pltpu.CompilerParams(vmem_limit_bytes=VMEM_BYTES),
        name="finish",
    )(received, lengths)
    return tuple(o.reshape(-1) for o in outs)


def per_device(n_req, n_tp, hidden_states, norm_gain, head, target_ids, lengths):
    rows = hidden_states.shape[0] // 2
    cw_pairs, ccw_pairs = ring_pairs(n_req, n_tp, 1), ring_pairs(n_req, n_tp, -1)
    other_core, other_y = tp_pairs(n_req, n_tp, 1), tp_pairs(n_req, n_tp, 2)
    sizes = (n_req, n_tp, rows)
    part = part_rows("y", rows)
    metas, stats = [], []

    def send(value, pairs):
        return lax.ppermute(value, AXES, pairs)

    def work(items, early=()):
        pieces, meta = zip(*items)
        stats.append(stats_of(pieces, meta, head, other_head, *sizes, early=early))
        metas.append(meta)

    def after(value):
        value, stats[-1] = lax.optimization_barrier((value, stats[-1]))
        return value

    other_head = send(head, other_core)
    xn, to_cw, to_ccw, early = norm_rows(
        hidden_states, norm_gain, target_ids, head, n_tp, rows
    )
    items = [(xn, ((0, 0, "all"),))]
    cw, ccw, late = to_cw, to_ccw, []
    for hops in range(1, n_req // 2 + 1):
        next_cw, next_ccw = send(cw, cw_pairs), send(ccw, ccw_pairs)
        others = []
        both = [(0, 0, part), (1, 0, part)]
        if hops == 2:
            (c_both,) = cut((cw, ccw), [[(0, part, part), (1, part, part)]])
            c_both = send(c_both, other_y)
            others = [(c_both, ((1, 1, "c"), (-1, 1, "c")))]
        elif hops > 2:
            (y_message,) = cut((cw, ccw), [both])
            y_next = send(y_message, other_y)
            if hops == 3:
                c_cw, c_ccw = cut((c_both,), [[both[0]], [(0, part, part)]])
            else:
                c_cw, c_ccw, _ = lax.optimization_barrier((c_cw, c_ccw, y_message))
            c_cw, c_ccw = send(c_cw, cw_pairs), send(c_ccw, ccw_pairs)
            others = late + [
                (c_cw, ((1, hops - 1, "c"),)),
                (c_ccw, ((-1, hops - 1, "c"),)),
                (y_next, ((1, hops - 1, "y"), (-1, hops - 1, "y"))),
            ]
            late = []
        work(items, () if stats else (early,))
        if hops == 2:
            (y_message,) = cut((cw, ccw), [both])
            late = [(send(y_message, other_y), ((1, 1, "y"), (-1, 1, "y")))]
        cw, ccw = after(next_cw), after(next_ccw)
        items = [(cw, ((1, hops, "half"),)), (ccw, ((-1, hops, "half"),))]
        if 2 * hops == n_req:
            work(items)
            items = []
        items += others
        if hops == 2:
            items, late = items + late, []
    pieces, meta = zip(*items)
    packed = stats_of(
        pieces, meta, head, other_head, *sizes, earlier=tuple(metas), stats=stats, tail=True
    )
    received = lax.all_to_all(packed, AXES, 0, 0, tiled=True)
    return finish(received, lengths)


def solution(mesh):
    n_req, n_tp = mesh.shape["req"], mesh.shape["tp"]
    in_specs = (P("req", None), P(), P(None, ("req", "tp")), P("req"), P("req"))
    out_specs = (P("req"), P("req"), P("req"), P("req"))
    return jax.shard_map(
        functools.partial(per_device, n_req, n_tp),
        mesh=mesh,
        in_specs=in_specs,
        out_specs=out_specs,
        check_vma=False,
    )
```
